32 devices in a mesh: wide: 16 (over z, y, x), narrow: 2 (over core).
Axes of the slice: x: 2, y: 2, z: 4, core: 2. Of those that a mesh axis runs over, the one named last changes fastest.
Arguments:
- context: bfloat16 [4096, 3072], P('wide', 'narrow'), may hold values from -6 to 6
- out_weight: bfloat16 [3072, 6144], P('wide', 'narrow'), may hold values from -0.109375 to 0.109375
- residual: bfloat16 [4096, 6144], P('wide', 'narrow'), may hold values from -180 to 180
- ln_gain: bfloat16 [6144], P('narrow'), may hold values from 0.5 to 1.5
- side_down: bfloat16 [6144, 768], P('narrow', 'wide'), may hold values from -0.078125 to 0.078125
- f_weight: bfloat16 [384, 384], replicated, may hold values from -0.3125 to 0.3125
- g_weight: bfloat16 [384, 384], replicated, may hold values from -0.3125 to 0.3125
- targets: float32 [4096, 768], P(('wide', 'narrow')), may hold values from -18 to 18
Outputs:
- side_out: float32 [4096, 768], P(('wide', 'narrow'))
- f_grad: float32 [384, 384], replicated
- g_grad: float32 [384, 384], replicated
The draws below stay inside these ranges and needn't reach their ends.
All inputs are finite; a program needn't handle non-finite values.
Results may differ from the reference program's by a relative error of at most 0.00035.
The reference program's roundings to bfloat16 on the way (of `stream` and `scaled`) count: a program that leaves them out, or rounds other values in their place, can miss the bound.
Values may be sent and summed in bfloat16 or wider, within the bound.
No kernel may reach another device: no remote copies, remote signals or barrier semaphores. Data moves between devices by JAX's collectives and lax.ppermute only.
A program may use at most 64 MiB of HBM per device.

```python
import math
import jax
import jax.numpy as jnp
from jax import lax

D = 6144
SIDE = 768
HD = 3072
HALF = 384
TOKENS = 4096


def draw_targets(key, part):
    first_key = jax.random.fold_in(key, 11)
    position = jnp.arange(TOKENS, dtype=jnp.float32) / max(TOKENS - 1, 1)
    rising = jnp.exp(position * jnp.log(3.0))
    base = jnp.clip(jax.random.normal(first_key, (TOKENS, SIDE), jnp.float32), -6.0, 6.0)
    return (base * rising[:, None]).astype(jnp.float32)


def draw_residual(key, part):
    noise_key = jax.random.fold_in(key, 31)
    row_key = jax.random.fold_in(key, 37)
    column_key = jax.random.fold_in(key, 41)
    shift_key = jax.random.fold_in(key, 43)
    feature = jnp.arange(D, dtype=jnp.float32) / max(D - 1, 1)
    rise = jnp.exp(feature * 0.6 * math.log(3.0))
    row_scale = jnp.exp(jax.random.uniform(row_key, (TOKENS,), jnp.float32, math.log(0.3), math.log(3.0)))
    noise = jnp.clip(jax.random.normal(noise_key, (TOKENS, D), jnp.float32), -4.0, 4.0)
    column_scale = jnp.exp(jax.random.uniform(column_key, (D,), jnp.float32, math.log(0.3), math.log(3.0))) * rise
    shift = jnp.clip(jax.random.normal(shift_key, (TOKENS,), jnp.float32), -2.5, 2.5)
    values = row_scale[:, None] * column_scale[None, :] * (noise + shift[:, None])
    return values.astype(jnp.bfloat16)


def block_scale(rng, shape, cuts, least, largest):
    factor_of, own = 1.0, jax.random.fold_in(rng, 6)
    for axis_at, blocks in cuts:
        steps = jnp.exp(jax.random.uniform(jax.random.fold_in(own, axis_at), (blocks,), jnp.float32, least / len(cuts), largest / len(cuts)))
        factor_of = factor_of * jnp.repeat(steps, shape[axis_at] // blocks).reshape([-1 if axis == axis_at else 1 for axis in range(len(shape))])
    return factor_of


def scatter_about(key, dims, width, reach, shards=(), kind=jnp.bfloat16):
    factor_of = block_scale(key, dims, shards, -0.22, 0.18) if shards else 1.0
    array = jax.random.normal(key, dims, jnp.float32) * width * factor_of
    return jnp.minimum(jnp.maximum(array, -reach), reach).astype(kind)


def setup_inputs(seed: int = 0) -> dict:
    seeds = jax.random.split(jax.random.key(seed), 9)
    context = scatter_about(seeds[0], (TOKENS, HD), 1.0, 6.0, ((0, 16), (1, 2)))
    out_weight = scatter_about(seeds[1], (HD, D), HD ** -0.5, 0.109375, ((0, 16), (1, 2)))
    residual = draw_residual(jax.random.fold_in(seeds[8], 71), 0)
    ln_gain = jnp.clip(1.0 + 0.1 * jax.random.normal(seeds[3], (D,), jnp.float32), 0.5, 1.5).astype(jnp.bfloat16)
    side_down = scatter_about(seeds[4], (D, SIDE), D ** -0.5, 0.078125, ((0, 2), (1, 16)))
    f_weight = scatter_about(seeds[5], (HALF, HALF), HALF ** -0.5, 0.3125)
    g_weight = scatter_about(seeds[6], (HALF, HALF), HALF ** -0.5, 0.3125)
    targets = draw_targets(jax.random.fold_in(seeds[8], 71), 0)
    return dict(context=context, out_weight=out_weight, residual=residual, ln_gain=ln_gain, side_down=side_down, f_weight=f_weight, g_weight=g_weight, targets=targets)


def coupling(values, weight):
    return jax.nn.gelu(jnp.dot(values, weight, precision=lax.Precision.HIGHEST))

def side_block(f_w, g_w, side_in):
    half = side_in.shape[1] // 2
    first = side_in[:, :half]
    second = side_in[:, half:]
    upper = first + coupling(second, f_w)
    lower = second + coupling(upper, g_w)
    return jnp.concatenate([upper, lower], axis=1)

def reference(context, out_weight, residual, ln_gain, side_down, f_weight, g_weight, targets):
    block_rows = min(1024, TOKENS)
    blocks = TOKENS // block_rows
    ctx_blocks = context.reshape(blocks, block_rows, context.shape[1])
    res_blocks = residual.reshape(blocks, block_rows, residual.shape[1])
    gain_value = ln_gain.astype(jnp.float32)
    gain_map = jnp.dot(ln_gain[None, :], side_down, preferred_element_type=jnp.float32)[0]

    def one_block(pair):
        ctx, res = pair
        attn_out = jnp.dot(ctx, out_weight, preferred_element_type=jnp.float32)
        stream = (res.astype(jnp.float32) + attn_out).astype(jnp.bfloat16)
        stream_value = stream.astype(jnp.float32)
        row_sum = lax.optimization_barrier(jnp.sum(stream_value, axis=1))
        row_squares = lax.optimization_barrier(jnp.sum(stream_value * stream_value, axis=1))
        scaled = (stream_value * gain_value[None, :]).astype(jnp.bfloat16)
        projected = jnp.dot(scaled, side_down, preferred_element_type=jnp.float32)
        mean = row_sum / D
        spread = row_squares / D - mean * mean
        return (projected - mean[:, None] * gain_map[None, :]) / jnp.sqrt(spread + 1e-06)[:, None]
    side_in = lax.map(one_block, (ctx_blocks, res_blocks)).reshape(TOKENS, side_down.shape[1])
    f_w = f_weight.astype(jnp.float32)
    g_w = g_weight.astype(jnp.float32)

    def loss_of(fw_value, gw_value):
        out = side_block(fw_value, gw_value, side_in)
        return 0.5 * jnp.sum((out - targets) ** 2) / TOKENS
    side_out = side_block(f_w, g_w, side_in)
    f_grad, g_grad = jax.grad(loss_of, argnums=(0, 1))(f_w, g_w)
    return (side_out, f_grad, g_grad)
```

```python
import functools

import jax
import jax.numpy as jnp
import numpy as np
from jax import lax
from jax.sharding import PartitionSpec as P

HIGH = lax.Precision.HIGH
F32 = jnp.float32
BF16 = jnp.bfloat16


def coupling(values, weight):
    return jax.nn.gelu(jnp.dot(values, weight, precision=HIGH))


def slot_table(planes):
    order = [sorted(range(planes), key=lambda p: (abs(p - at), p)) for at in range(planes)]
    place = [[row.index(p) for p in range(planes)] for row in order]
    return order, place


def per_device(group, wides, narrows, context, out_weight, residual, ln_gain, side_down, f_weight, g_weight, targets):
    planes = wides // group
    wide, core = lax.axis_index("wide"), lax.axis_index("narrow")
    plane, member = wide // group, wide % group
    order, place = slot_table(planes)
    short = planes <= 4
    if not short:
        order = place = [list(range(planes))] * planes

    def to_member(value, s):
        pairs = [(i, i - i % group + (i % group ^ s)) for i in range(wides)]
        return lax.ppermute(value, "wide", pairs) if s else value

    def to_core(value, t):
        return lax.ppermute(value, "narrow", [(i, i ^ t) for i in range(narrows)]) if t else value

    def along(value):
        if not short:
            lines = [[p * group + m for p in range(planes)] for m in range(group)]
            return list(lax.all_gather(value, "wide", axis_index_groups=lines))
        up, down = [value], [value]
        for _ in range(planes - 1):
            up.append(lax.ppermute(up[-1], "wide", [(i, i + group) for i in range(wides - group)]))
            down.append(lax.ppermute(down[-1], "wide", [(i + group, i) for i in range(wides - group)]))
        slots = [value]
        for j in range(1, planes):
            found, which, table = [], {}, []
            for at in range(planes):
                step = at - order[at][j]
                if step not in which:
                    which[step] = len(found)
                    found.append(up[step] if step > 0 else down[-step])
                table.append(which[step])
            at = jnp.asarray(np.array(table, np.int32))[plane]
            choice = found[0]
            for i in range(1, len(found)):
                choice = jnp.where(at == i, found[i], choice)
            slots.append(choice)
        return slots

    def block(value, index, size, axis):
        return lax.dynamic_slice_in_dim(value, index * size, size, axis)

    slot_plane = jnp.asarray(np.array(order, np.int32))[plane]
    features = out_weight.shape[1] // group
    rows = out_weight.shape[0]
    tokens = context.shape[0]
    members = range(group)

    pieces = [to_member(block(out_weight, member ^ s, features, 1), s) for s in members]
    lines = [along(piece) for piece in pieces]
    downs = [to_member(block(side_down.T, member ^ s, features, 1), s) for s in members]
    columns = downs[0].shape[0]
    down_plane = jnp.zeros((group * columns, features), BF16)
    for s in members:
        down_plane = lax.dynamic_update_slice_in_dim(down_plane, downs[s], (member ^ s) * columns, 0)
    down_slots = along(down_plane)

    part = jnp.concatenate([to_member(context, s) for s in members], axis=0)
    parts = [to_core(part, t) for t in range(narrows)]
    stay = jnp.concatenate([to_member(block(residual, member ^ s, features, 1), s) for s in members], axis=0)

    weight = jnp.zeros((wides * rows, features), BF16)
    for j in range(planes):
        for s in members:
            at = (slot_plane[j] * group + (member ^ s)) * rows
            weight = lax.dynamic_update_slice_in_dim(weight, lines[s][j], at, 0)
    attn_sum = jnp.zeros((), F32)
    for t in range(narrows):
        attn_sum = attn_sum + jnp.dot(
            parts[t], block(weight, core ^ t, part.shape[1], 0), preferred_element_type=F32
        )
    stream = (stay.astype(F32) + attn_sum).astype(BF16)
    stream_value = stream.astype(F32)
    gain = block(ln_gain, member, features, 0)
    scaled = (stream_value * gain.astype(F32)[None, :]).astype(BF16)

    local = tokens // narrows
    stats = jnp.stack([jnp.sum(stream_value, axis=1), jnp.sum(stream_value * stream_value, axis=1)])
    stats = stats.reshape(2, group, narrows, local)

    def sum_cores(pick):
        total = pick(core)
        for t in range(1, narrows):
            total = total + to_core(pick(core ^ t), t)
        return total

    def sum_members(pick):
        total = pick(0)
        for s in range(1, group):
            total = total + to_member(pick(s), s)
        return total

    stats = sum_cores(lambda k: lax.dynamic_index_in_dim(stats, k, 2, keepdims=False))
    stats = sum_members(lambda s: stats[:, s])

    gain_rows = jnp.broadcast_to(gain[None, :], (8, features))
    dims = (((1,), (1,)), ((), ()))

    def project(down):
        value = lax.dot_general(scaled, down, dims, preferred_element_type=F32)
        gain_part = lax.dot_general(gain_rows, down, dims, preferred_element_type=F32)
        value = value.reshape(group, narrows, local, value.shape[1])

        def pick(k):
            mine = lax.dynamic_index_in_dim(value, k, 1, keepdims=False)
            return jnp.concatenate([mine.reshape(group * local, -1), gain_part], axis=0)

        summed = sum_cores(pick)
        tail = summed[group * local :]
        return sum_members(lambda s: jnp.concatenate([summed[s * local : (s + 1) * local], tail], axis=0))

    if short:
        projected = [project(down) for down in down_slots]
    else:
        projected = jnp.split(project(jnp.concatenate(down_slots, axis=0)), planes, axis=1)
    ordered = []
    for p in range(planes):
        at = jnp.asarray(np.array([row[p] for row in place], np.int32))[plane]
        choice = projected[0]
        for j in range(1, planes):
            choice = jnp.where(at == j, projected[j], choice)
        ordered.append(choice)
    ordered = jnp.concatenate(ordered, axis=1)
    gain_map = ordered[local]
    projected = ordered[:local]

    width = out_weight.shape[1] * narrows
    mean = stats[0] / width
    spread = stats[1] / width - mean * mean
    side_in = (projected - mean[:, None] * gain_map[None, :]) / jnp.sqrt(spread + 1e-06)[:, None]
    half = side_in.shape[1] // 2
    f_w, g_w = f_weight.astype(F32), g_weight.astype(F32)
    first, second = side_in[:, :half], side_in[:, half:]
    f_value, f_pull = jax.vjp(coupling, second, f_w)
    upper = first + f_value
    g_value, g_pull = jax.vjp(coupling, upper, g_w)
    lower = second + g_value
    side_out = jnp.concatenate([upper, lower], axis=1)
    misfit = (side_out - targets) / (local * wides * narrows)
    upper_back, g_local = g_pull(misfit[:, half:])
    f_local = f_pull(misfit[:, :half] + upper_back)[1]

    if (2 * half) % (wides * narrows * 8):
        f_total, g_total = lax.psum((f_local, g_local), ("wide", "narrow"))
        return side_out, f_total, g_total

    grads = jnp.concatenate([f_local, g_local], axis=0)
    share = 2 * half // narrows
    grads = sum_cores(lambda k: block(grads, k, share, 0))
    share = share // group
    part = grads
    grads = sum_members(lambda s: block(part, member ^ s, share, 0))
    share = share // planes

    def shift(value, k):
        return lax.ppermute(value, "wide", [(i, (i + k * group) % wides) for i in range(wides)])

    part = grads
    grads = block(part, plane, share, 0)
    for k in range(1, planes):
        grads = grads + shift(block(part, (plane + k) % planes, share, 0), k)
    whole = jnp.zeros((planes * share, half), F32)
    for k in range(planes):
        piece = shift(grads, k) if k else grads
        whole = lax.dynamic_update_slice_in_dim(whole, piece, (plane - k) % planes * share, 0)
    share = share * planes
    part, whole = whole, jnp.zeros((group * share, half), F32)
    for s in members:
        whole = lax.dynamic_update_slice_in_dim(whole, to_member(part, s), (member ^ s) * share, 0)
    share = share * group
    part, whole = whole, jnp.zeros((narrows * share, half), F32)
    for t in range(narrows):
        whole = lax.dynamic_update_slice_in_dim(whole, to_core(part, t), (core ^ t) * share, 0)
    return side_out, whole[:half], whole[half:]


def solution(mesh):
    wides, narrows = mesh.shape["wide"], mesh.shape["narrow"]
    group = 4 if wides % 4 == 0 else 1
    in_specs = (
        P("wide", "narrow"),
        P("wide", "narrow"),
        P("wide", "narrow"),
        P("narrow"),
        P("narrow", "wide"),
        P(),
        P(),
        P(("wide", "narrow"), None),
    )
    out_specs = (P(("wide", "narrow"), None), P(), P())
    return jax.shard_map(
        functools.partial(per_device, group, wides, narrows),
        mesh=mesh,
        in_specs=in_specs,
        out_specs=out_specs,
        check_vma=False,
    )
```

```python
import functools

import jax
import jax.numpy as jnp
from jax import lax
from jax.experimental import pallas as pl
from jax.experimental.pallas import tpu as pltpu
from jax.sharding import PartitionSpec as P

HIGH = lax.Precision.HIGH
F32 = jnp.float32
BF16 = jnp.bfloat16


def coupling(values, weight):
    return jax.nn.gelu(jnp.dot(values, weight, precision=HIGH))


def attend_kernel(group, planes, count, *refs):
    mine_ref, other_ref, *refs = refs
    stay_refs, refs = refs[:group], refs[group:]
    gain_ref, *refs = refs
    flow_refs, (scaled_ref, stats_ref, weight, sems) = refs[:-4], refs[-4:]
    own, up, down = flow_refs[:2], flow_refs[2 : 2 * planes], flow_refs[2 * planes :]
    wide, core = lax.axis_index("wide"), lax.axis_index("narrow")
    plane, member = wide // group, wide % group
    rows = own[0].shape[0]

    def copies(at, p):
        if at == p:
            first, rest = own
        else:
            first, rest = (up if at > p else down)[2 * (abs(at - p) - 1) :][:2]
        out = []
        for s in range(group):
            source = rest.at[pl.ds((s - 1) * rows, rows)] if s else first
            target = pl.multiple_of((p * group + (member ^ s)) * rows, 64)
            out.append(pltpu.make_async_copy(source, weight.at[pl.ds(target, rows)], sems.at[p, s]))
        return out

    for at in range(planes):

        @pl.when((pl.program_id(0) == 0) & (plane == at))
        def _():
            everything = [copy for p in range(planes) for copy in copies(at, p)]
            for copy in everything:
                copy.start()
            for copy in everything:
                copy.wait()

    heads = mine_ref.shape[2]
    local = mine_ref.shape[1]
    gain = gain_ref[...].astype(F32)
    for h in range(0, group, 2):
        lhs = mine_ref[h : h + 2].reshape(2 * local, heads)
        rhs = other_ref[h : h + 2].reshape(2 * local, heads)
        at = pl.multiple_of(core * heads, 128)
        total = jnp.dot(lhs, weight[pl.ds(at, heads)], preferred_element_type=F32)
        at = pl.multiple_of((1 - core) * heads, 128)
        total += jnp.dot(rhs, weight[pl.ds(at, heads)], preferred_element_type=F32)
        stay = jnp.concatenate([stay_refs[h][...], stay_refs[h + 1][...]], axis=0)
        stream = (stay.astype(F32) + total).astype(BF16).astype(F32)
        scaled_ref[0, h * local : (h + 2) * local] = (stream * gain).astype(BF16)
        sums = jnp.sum(stream, axis=1, keepdims=True)
        squares = jnp.sum(stream * stream, axis=1, keepdims=True)
        lane = lax.broadcasted_iota(jnp.int32, (2 * local, 128), 1)
        both = jnp.where(lane == 0, sums, jnp.where(lane == 1, squares, 0.0))
        stats_ref[:, h * local : (h + 2) * local] = both.T[:8]
    scaled_ref[0, group * local :] = jnp.broadcast_to(gain_ref[...], (16, count))


def attend(mine, other, stay, gain, own, up, down):
    group, tokens, heads = mine.shape
    local = tokens // 2
    count = gain.shape[1]
    planes = len(up) + 1
    flow = [*own] + [v for pair in up for v in pair] + [v for pair in down for v in pair]
    whole = pl.BlockSpec(memory_space=pl.ANY)
    part = pl.BlockSpec((group, local, heads), lambda i: (0, i, 0))
    work = group * tokens * heads * 2 * count
    return pl.pallas_call(
        functools.partial(attend_kernel, group, planes, count),
        grid=(2,),
        in_specs=[part, part]
        + [pl.BlockSpec((local, count), lambda i: (i, 0))] * group
        + [pl.BlockSpec((1, count), lambda i: (0, 0))]
        + [whole] * len(flow),
        out_specs=[
            pl.BlockSpec((1, group * local + 16, count), lambda i: (i, 0, 0)),
            pl.BlockSpec((8, group * local), lambda i: (0, i)),
        ],
        out_shape=[
            jax.ShapeDtypeStruct((2, group * local + 16, count), BF16),
            jax.ShapeDtypeStruct((8, group * tokens), F32),
        ],
        scratch_shapes=[
            pltpu.VMEM((2 * heads, count), BF16),
            pltpu.SemaphoreType.DMA((planes, group)),
        ],
        compiler_params=pltpu.CompilerParams(vmem_limit_bytes=60 << 20),
        cost_estimate=pl.CostEstimate(flops=2 * work, bytes_accessed=14 << 20, transcendentals=0),
    )(mine, other, *stay, gain, *flow)


def project_kernel(group, planes, *refs):
    scaled_ref, stats_ref, *refs = refs
    flow_refs, (out_ref, down, sems) = refs[:-3], refs[-3:]
    own, up, lower = flow_refs[0], flow_refs[1:planes], flow_refs[planes:]
    plane, core = lax.axis_index("wide") // group, lax.axis_index("narrow")
    rows = own.shape[0]

    def copies(at):
        out = []
        for p in range(planes):
            source = own if at == p else (up if at > p else lower)[abs(at - p) - 1]
            out.append(pltpu.make_async_copy(source, down.at[pl.ds(p * rows, rows)], sems.at[p]))
        return out

    for at in range(planes):

        @pl.when(plane == at)
        def _():
            for copy in copies(at):
                copy.start()
            for copy in copies(at):
                copy.wait()

    local = (scaled_ref.shape[1] - 16) // group
    span = local + 8
    dims = (((1,), (1,)), ((), ()))
    gain = lax.dot_general(
        scaled_ref[0, group * local : group * local + 16], down[...], dims, preferred_element_type=F32
    )
    for t in range(2):
        k = core if t == 0 else 1 - core
        at = pl.multiple_of(k * (group * local), 128)
        value = lax.dot_general(scaled_ref[k, : group * local], down[...], dims, preferred_element_type=F32)
        sums = stats_ref[:, pl.ds(at, group * local)]
        for s in range(group):
            out_ref[t, s * span : s * span + local] = value[s * local : (s + 1) * local]
            out_ref[t, s * span + local : (s + 1) * span] = gain[:8]
            out_ref[t, s * span + local + 1 : s * span + local + 3, :local] = sums[:2, s * local : (s + 1) * local]


def project(group, scaled, stats, own, up, down):
    planes = len(up) + 1
    rows, features = own.shape
    local = (scaled.shape[1] - 16) // group
    count = planes * rows
    whole = pl.BlockSpec(memory_space=pl.ANY)
    inside = pl.BlockSpec(memory_space=pltpu.VMEM)
    return pl.pallas_call(
        functools.partial(project_kernel, group, planes),
        in_specs=[inside, inside] + [whole] * (2 * planes - 1),
        out_specs=inside,
        out_shape=jax.ShapeDtypeStruct((2, group * (local + 8), count), F32),
        scratch_shapes=[pltpu.VMEM((count, features), BF16), pltpu.SemaphoreType.DMA((planes,))],
        compiler_params=pltpu.CompilerParams(vmem_limit_bytes=40 << 20),
        cost_estimate=pl.CostEstimate(
            flops=4 * group * local * features * count, bytes_accessed=8 << 20, transcendentals=0
        ),
    )(scaled, stats, own, *up, *down)


def per_device(group, wides, narrows, context, out_weight, residual, ln_gain, side_down, f_weight, g_weight, targets):
    planes = wides // group
    wide, core = lax.axis_index("wide"), lax.axis_index("narrow")
    plane, member = wide // group, wide % group
    short = planes == 4 and narrows == 2
    features = out_weight.shape[1] // group
    rows = out_weight.shape[0]
    tokens = context.shape[0]
    local = tokens // narrows
    members = range(group)
    cores = range(narrows)

    def to_member(value, s):
        pairs = [(i, i - i % group + (i % group ^ s)) for i in range(wides)]
        return lax.ppermute(value, "wide", pairs) if s else value

    def to_core(value, t):
        return lax.ppermute(value, "narrow", [(i, i ^ t) for i in range(narrows)]) if t else value

    def block(value, index, size, axis):
        return lax.dynamic_slice_in_dim(value, index * size, size, axis)

    def step_up(value, k):
        pairs = [(i, i + group) for i in range((k - 1) * group, wides - group)]
        return lax.ppermute(value, "wide", pairs)

    def step_down(value, k):
        pairs = [(i + group, i) for i in range(wides - k * group)]
        return lax.ppermute(value, "wide", pairs)

    def sum_cores(pick):
        total = pick(core)
        for t in range(1, narrows):
            total = total + to_core(pick(core ^ t), t)
        return total

    def sum_members(pick):
        total = pick(0)
        for s in range(1, group):
            total = total + to_member(pick(s), s)
        return total

    own = [block(out_weight, member ^ s, features, 1) for s in members]
    down_own = [block(side_down.T, member ^ s, features, 1) for s in members]
    stay_own = [block(residual, member ^ s, features, 1) for s in members]
    gain = block(ln_gain, member, features, 0)[None, :]
    columns = down_own[0].shape[0]
    side_rows = group * local

    def in_plane(downs):
        value = jnp.zeros((group * columns, features), BF16)
        for s in members:
            value = lax.dynamic_update_slice_in_dim(value, downs[s], (member ^ s) * columns, 0)
        return value

    if short:
        up, down = [[v] for v in own[:1]], [[v] for v in own[:1]]

        def pass_on(i, k):
            up[i].append(step_up(up[i][-1], k))
            down[i].append(step_down(down[i][-1], k))

        pass_on(0, 1)
        pass_on(0, 2)
        pieces = [to_member(own[s], s) for s in members]
        rest = jnp.concatenate(pieces[1:], axis=0)

        rest, context, down_own, up, down = lax.optimization_barrier((rest, context, down_own, up, down))
        up.append([rest])
        down.append([rest])
        pass_on(1, 1)
        pass_on(0, 3)
        arrived = [context, to_member(context, 1), to_member(context, 2)]
        down_plane = in_plane([to_member(down_own[s], s) for s in members])

        state = (down_plane, arrived, stay_own, up, down)
        down_plane, arrived, stay_own, up, down = lax.optimization_barrier(state)
        up.append([down_plane])
        down.append([down_plane])
        pass_on(1, 2)
        pass_on(2, 1)
        arrived.append(to_member(arrived[0], 3))
        stay = [stay_own[0], None, None, to_member(stay_own[3], 3)]
        part = jnp.concatenate(arrived, axis=0)

        part, stay_own, up, down = lax.optimization_barrier((part, stay_own, up, down))
        pass_on(1, 3)
        pass_on(2, 2)
        stay[1], stay[2] = to_member(stay_own[1], 1), to_member(stay_own[2], 2)
        mine, other = [v.reshape(group, tokens, -1) for v in (part, to_core(part, 1))]

        mine, other, stay, up, down = lax.optimization_barrier((mine, other, stay, up, down))
        pass_on(2, 3)
        pairs = [list(zip(v[0][1:], v[1][1:])) for v in (up, down)]
        scaled, stats = attend(mine, other, stay, gain, [own[0], rest], *pairs)
        both = project(group, scaled, stats, down_plane, up[2][1:], down[2][1:])
        summed = both[0] + to_core(both[1], 1)
        span = local + 8
        projected = summed[:span]
        for s in range(1, group):
            projected = projected + to_member(summed[s * span : (s + 1) * span], s)
        stats = projected[local + 1 : local + 3, :local]
    else:
        pieces = [to_member(own[s], s) for s in members]
        down_plane = in_plane([to_member(down_own[s], s) for s in members])
        arrived = [to_member(context, s) for s in members]
        stay = [to_member(stay_own[s], s) for s in members]
        parts = [to_core(jnp.concatenate(arrived, axis=0), t) for t in cores]
        lines = [[p * group + m for p in range(planes)] for m in range(group)]
        chunk = jnp.zeros((group * rows, features), BF16)
        for s in members:
            chunk = lax.dynamic_update_slice_in_dim(chunk, pieces[s], (member ^ s) * rows, 0)
        weight = lax.all_gather(chunk, "wide", axis_index_groups=lines, tiled=True)
        all_down = lax.all_gather(down_plane, "wide", axis_index_groups=lines, tiled=True)

        def by_core(value):
            value = value.reshape(group, narrows, local, -1)
            return value.swapaxes(0, 1).reshape(group * tokens, -1)

        heads = context.shape[1]
        attn_sum = jnp.zeros((), F32)
        for t in cores:
            share = block(weight, core ^ t, heads, 0)
            attn_sum = attn_sum + jnp.dot(parts[t], share, preferred_element_type=F32)
        stream = (jnp.concatenate(stay, axis=0).astype(F32) + attn_sum).astype(BF16)
        stream = by_core(stream).astype(F32)
        scaled = (stream * gain.astype(F32)).astype(BF16).reshape(narrows, side_rows, features)
        gains = jnp.broadcast_to(gain[None], (narrows, 8, features))
        scaled = jnp.concatenate([scaled, gains], axis=1)
        stats = jnp.stack([jnp.sum(stream, axis=1), jnp.sum(stream * stream, axis=1)])
        stats_own = stats.reshape(2, narrows, group, local)

        def share_of_core(k):
            lhs = lax.dynamic_index_in_dim(scaled, k, 0, keepdims=False)
            return lax.dot_general(lhs, all_down, (((1,), (1,)), ((), ())), preferred_element_type=F32)

        summed = sum_cores(share_of_core)
        tail = summed[side_rows:]
        projected = sum_members(
            lambda s: jnp.concatenate([summed[s * local : (s + 1) * local], tail], axis=0)
        )
        summed_stats = sum_cores(lambda k: lax.dynamic_index_in_dim(stats_own, k, 1, keepdims=False))
        stats = sum_members(lambda s: summed_stats[:, s])
    projected, gain_map = projected[:local], projected[local]

    width = out_weight.shape[1] * narrows
    mean = stats[0] / width
    spread = stats[1] / width - mean * mean
    side_in = (projected - mean[:, None] * gain_map[None, :]) / jnp.sqrt(spread + 1e-06)[:, None]
    half = side_in.shape[1] // 2
    f_w, g_w = f_weight.astype(F32), g_weight.astype(F32)
    first, second = side_in[:, :half], side_in[:, half:]
    f_value, f_pull = jax.vjp(coupling, second, f_w)
    upper = first + f_value
    g_value, g_pull = jax.vjp(coupling, upper, g_w)
    lower = second + g_value
    side_out = jnp.concatenate([upper, lower], axis=1)
    misfit = (side_out - targets) / (local * wides * narrows)
    upper_back, g_local = g_pull(misfit[:, half:])
    f_local = f_pull(misfit[:, :half] + upper_back)[1]

    if (2 * half) % (wides * narrows * 8):
        f_total, g_total = lax.psum((f_local, g_local), ("wide", "narrow"))
        return side_out, f_total, g_total

    grads = jnp.concatenate([f_local, g_local], axis=0)
    share = 2 * half // narrows
    grads = sum_cores(lambda k: block(grads, k, share, 0))
    share = share // group
    part = grads
    grads = sum_members(lambda s: block(part, member ^ s, share, 0))
    share = share // planes

    def shift(value, k):
        return lax.ppermute(value, "wide", [(i, (i + k * group) % wides) for i in range(wides)])

    part = grads
    grads = block(part, plane, share, 0)
    for k in range(1, planes):
        grads = grads + shift(block(part, (plane + k) % planes, share, 0), k)
    whole = jnp.zeros((planes * share, half), F32)
    for k in range(planes):
        piece = shift(grads, k) if k else grads
        whole = lax.dynamic_update_slice_in_dim(whole, piece, (plane - k) % planes * share, 0)
    share = share * planes
    part, whole = whole, jnp.zeros((group * share, half), F32)
    for s in members:
        whole = lax.dynamic_update_slice_in_dim(whole, to_member(part, s), (member ^ s) * share, 0)
    share = share * group
    part, whole = whole, jnp.zeros((narrows * share, half), F32)
    for t in range(narrows):
        whole = lax.dynamic_update_slice_in_dim(whole, to_core(part, t), (core ^ t) * share, 0)
    return side_out, whole[:half], whole[half:]


def solution(mesh):
    wides, narrows = mesh.shape["wide"], mesh.shape["narrow"]
    group = 4 if wides % 4 == 0 else 1
    in_specs = (
        P("wide", "narrow"),
        P("wide", "narrow"),
        P("wide", "narrow"),
        P("narrow"),
        P("narrow", "wide"),
        P(),
        P(),
        P(("wide", "narrow"), None),
    )
    out_specs = (P(("wide", "narrow"), None), P(), P())
    return jax.shard_map(
        functools.partial(per_device, group, wides, narrows),
        mesh=mesh,
        in_specs=in_specs,
        out_specs=out_specs,
        check_vma=False,
    )
```

```python
import functools

import jax
import jax.numpy as jnp
from jax import lax
from jax.experimental import pallas as pl
from jax.experimental.pallas import tpu as pltpu
from jax.sharding import PartitionSpec as P

HIGH = lax.Precision.HIGH
F32 = jnp.float32
BF16 = jnp.bfloat16
GROUP = 4


def coupling(values, weight):
    return jax.nn.gelu(jnp.dot(values, weight, precision=HIGH))


def place():
    wide, core = lax.axis_index("wide"), lax.axis_index("narrow")
    return wide // GROUP, wide % GROUP, core


def part_of(flow, at, p):
    steps = (len(flow) // 2 - 2) // 2
    step = abs(at - p)
    if step > steps:
        return flow[2:4]
    if not step:
        return flow[:2]
    first = 4 + 2 * (step - 1) + (0 if at > p else 2 * steps)
    return flow[first : first + 2]


def share_of(pair, s, start, count, span):
    at = start + (s - 1) * span if s else start
    return pair[1 if s else 0].at[pl.ds(at, count)]


def attend_kernel(rows, planes, *refs):
    mine_ref, other_ref, *flow, out_ref, weight, sems = refs
    plane, member, core = place()
    span = flow[0].shape[0]
    steps = (len(flow) // 2 - 2) // 2

    for at in range(planes):

        @pl.when((pl.program_id(0) == 0) & (plane == at))
        def _():
            copies = []
            for p in range(planes):
                if abs(at - p) > steps:
                    weight[p * GROUP * rows : (p + 1) * GROUP * rows] = jnp.zeros((GROUP * rows, weight.shape[1]), BF16)
                    continue
                for s in range(GROUP):
                    target = pl.multiple_of((p * GROUP + (member ^ s)) * rows, 64)
                    source = share_of(part_of(flow, at, p), s, 0, rows, span)
                    copies.append(pltpu.make_async_copy(source, weight.at[pl.ds(target, rows)], sems.at[p, s]))
            for copy in copies:
                copy.start()
            for copy in copies:
                copy.wait()

    group, local, heads = mine_ref.shape
    for h in range(0, group, 2):
        lhs = mine_ref[h : h + 2].reshape(2 * local, heads)
        rhs = other_ref[h : h + 2].reshape(2 * local, heads)
        at = pl.multiple_of(core * heads, 128)
        total = jnp.dot(lhs, weight[pl.ds(at, heads)], preferred_element_type=F32)
        at = pl.multiple_of((1 - core) * heads, 128)
        total += jnp.dot(rhs, weight[pl.ds(at, heads)], preferred_element_type=F32)
        out_ref[h * local : (h + 2) * local] = total


def attend(rows, planes, mine, other, flow):
    group, tokens, heads = mine.shape
    count = flow[0].shape[1]
    part = pl.BlockSpec((group, tokens // 2, heads), lambda i: (0, i, 0))
    return pl.pallas_call(
        functools.partial(attend_kernel, rows, planes),
        grid=(2,),
        in_specs=[part, part] + [pl.BlockSpec(memory_space=pl.ANY)] * len(flow),
        out_specs=pl.BlockSpec((group * tokens // 2, count), lambda i: (i, 0)),
        out_shape=jax.ShapeDtypeStruct((group * tokens, count), F32),
        scratch_shapes=[pltpu.VMEM((2 * heads, count), BF16), pltpu.SemaphoreType.DMA((planes, group))],
        compiler_params=pltpu.CompilerParams(vmem_limit_bytes=40 << 20),
        cost_estimate=pl.CostEstimate(
            flops=4 * group * tokens * heads * count, bytes_accessed=16 << 20, transcendentals=0
        ),
    )(mine, other, *flow)


def finish_kernel(rows, planes, *refs):
    total_ref, far_ref, gain_ref, *refs = refs
    stay_refs, (*flow, out_ref, weight, down, scaled, sums, sems, down_sems) = refs[:GROUP], refs[GROUP:]
    plane, member, core = place()
    span = flow[0].shape[0]
    columns = span - rows

    def far_copies():
        out = []
        for s in range(GROUP):
            target = pl.multiple_of((member ^ s) * rows, 64)
            source = share_of(flow[2:4], s, 0, rows, span)
            out.append(pltpu.make_async_copy(source, weight.at[pl.ds(target, rows)], sems.at[s]))
        return out

    def down_copies(at):
        out = []
        for p in range(planes):
            for s in range(GROUP):
                target = pl.multiple_of((p * GROUP + (member ^ s)) * columns, 16)
                source = share_of(part_of(flow, at, p), s, rows, columns, span)
                out.append(pltpu.make_async_copy(source, down.at[pl.ds(target, columns)], down_sems.at[p, s]))
        return out

    far = far_copies()
    for copy in far:
        copy.start()
    for at in range(planes):

        @pl.when(plane == at)
        def _():
            copies = down_copies(at)
            for copy in copies:
                copy.start()
            for copy in copies:
                copy.wait()

    for copy in far:
        copy.wait()
    local = stay_refs[0].shape[0] // 2
    half = GROUP * local
    gain = gain_ref[...].astype(F32)
    for i in range(2):
        for h in range(0, GROUP, 2):
            at = i * half + h * local
            lhs = jnp.concatenate([far_ref[h + g, i * local : (i + 1) * local] for g in range(2)], axis=0)
            total = total_ref[at : at + 2 * local] + jnp.dot(lhs, weight[...], preferred_element_type=F32)
            stay = jnp.concatenate([stay_refs[h + g][i * local : (i + 1) * local] for g in range(2)], axis=0)
            stream = (stay.astype(F32) + total).astype(BF16).astype(F32)
            scaled[at : at + 2 * local] = (stream * gain).astype(BF16)
            row_sum = jnp.sum(stream, axis=1, keepdims=True)
            squares = jnp.sum(stream * stream, axis=1, keepdims=True)
            lane = lax.broadcasted_iota(jnp.int32, (2 * local, 128), 1)
            both = jnp.where(lane == 0, row_sum, jnp.where(lane == 1, squares, 0.0))
            sums[:, at : at + 2 * local] = both.T[:8]

    dims = (((1,), (1,)), ((), ()))
    gains = jnp.broadcast_to(gain_ref[...], (16, gain_ref.shape[1]))
    gains = lax.dot_general(gains, down[...], dims, preferred_element_type=F32)
    line = local + 8
    for t in range(2):
        k = core if t == 0 else 1 - core
        at = pl.multiple_of(k * half, 128)
        value = lax.dot_general(scaled[pl.ds(at, half)], down[...], dims, preferred_element_type=F32)
        stats = sums[:, pl.ds(at, half)]
        for s in range(GROUP):
            out_ref[t, s * line : s * line + local] = value[s * local : (s + 1) * local]
            out_ref[t, s * line + local : (s + 1) * line] = gains[:8]
            out_ref[t, s * line + local + 1 : s * line + local + 3, :local] = stats[:2, s * local : (s + 1) * local]


def finish(rows, planes, total, far, gain, stay, flow):
    count = total.shape[1]
    tokens = total.shape[0]
    span = flow[0].shape[0]
    out = (span - rows) * GROUP * planes
    inside = pl.BlockSpec(memory_space=pltpu.VMEM)
    return pl.pallas_call(
        functools.partial(finish_kernel, rows, planes),
        in_specs=[inside] * (3 + GROUP) + [pl.BlockSpec(memory_space=pl.ANY)] * len(flow),
        out_specs=inside,
        out_shape=jax.ShapeDtypeStruct((2, tokens // 2 + 8 * GROUP, out), F32),
        scratch_shapes=[
            pltpu.VMEM((GROUP * rows, count), BF16),
            pltpu.VMEM((out, count), BF16),
            pltpu.VMEM((tokens, count), BF16),
            pltpu.VMEM((8, tokens), F32),
            pltpu.SemaphoreType.DMA((GROUP,)),
            pltpu.SemaphoreType.DMA((planes, GROUP)),
        ],
        compiler_params=pltpu.CompilerParams(vmem_limit_bytes=40 << 20),
        cost_estimate=pl.CostEstimate(
            flops=2 * tokens * count * (GROUP * rows + out), bytes_accessed=16 << 20, transcendentals=0
        ),
    )(total, far, gain, *stay, *flow)


def per_device(group, wides, narrows, context, out_weight, residual, ln_gain, side_down, f_weight, g_weight, targets):
    planes = wides // group
    wide, core = lax.axis_index("wide"), lax.axis_index("narrow")
    plane, member = wide // group, wide % group
    short = group == GROUP and planes == 4 and narrows == 2
    features = out_weight.shape[1] // group
    rows = out_weight.shape[0]
    tokens = context.shape[0]
    local = tokens // narrows
    members = range(group)
    cores = range(narrows)

    def to_member(value, s):
        pairs = [(i, i - i % group + (i % group ^ s)) for i in range(wides)]
        return lax.ppermute(value, "wide", pairs) if s else value

    def to_core(value, t):
        return lax.ppermute(value, "narrow", [(i, i ^ t) for i in range(narrows)]) if t else value

    def block(value, index, size, axis):
        return lax.dynamic_slice_in_dim(value, index * size, size, axis)

    def step_up(value, k):
        pairs = [(i, i + group) for i in range((k - 1) * group, wides - group)]
        return lax.ppermute(value, "wide", pairs)

    def step_down(value, k):
        pairs = [(i + group, i) for i in range(wides - k * group)]
        return lax.ppermute(value, "wide", pairs)

    def sum_cores(pick):
        total = pick(core)
        for t in range(1, narrows):
            total = total + to_core(pick(core ^ t), t)
        return total

    def sum_members(pick):
        total = pick(0)
        for s in range(1, group):
            total = total + to_member(pick(s), s)
        return total

    own = [block(out_weight, member ^ s, features, 1) for s in members]
    down_own = [block(side_down.T, member ^ s, features, 1) for s in members]
    stay_own = [block(residual, member ^ s, features, 1) for s in members]
    gain = block(ln_gain, member, features, 0)[None, :]
    columns = down_own[0].shape[0]
    side_rows = group * local

    def in_plane(downs):
        value = jnp.zeros((group * columns, features), BF16)
        for s in members:
            value = lax.dynamic_update_slice_in_dim(value, downs[s], (member ^ s) * columns, 0)
        return value

    if short:
        own = [jnp.concatenate(pair, axis=0) for pair in zip(own, down_own)]
        boxes = [jnp.concatenate([context, value], axis=1) for value in stay_own[1:]]
        up, down = [[v] for v in own[:1]], [[v] for v in own[:1]]
        far = []

        def pass_on(i, k):
            up[i].append(step_up(up[i][-1], k))
            down[i].append(step_down(down[i][-1], k))

        def pass_last(i):
            middle = planes // 2 * group
            pairs = [(j, j + group) for j in range(wides - 2 * group, wides - group)]
            pairs += [(j + group, j) for j in range(group)]
            far.append(lax.ppermute(jnp.where(wide >= middle, up[i][-1], down[i][-1]), "wide", pairs))

        pass_on(0, 1)
        pass_on(0, 2)
        pieces = [to_member(own[s], s) for s in range(1, group)]
        rest = jnp.concatenate(pieces, axis=0)

        rest, boxes, up, down = lax.optimization_barrier((rest, boxes, up, down))
        up.append([rest])
        down.append([rest])
        pass_on(1, 1)
        pass_last(0)
        arrived = [to_member(boxes[0], 1), to_member(boxes[1], 2)]

        arrived, boxes, up, down, far = lax.optimization_barrier((arrived, boxes, up, down, far))
        pass_on(1, 2)
        arrived.append(to_member(boxes[2], 3))
        heads = context.shape[1]
        part = jnp.concatenate([context] + [v[:, :heads] for v in arrived], axis=0)
        stay = stay_own[:1] + [v[:, heads:] for v in arrived]

        part, stay, up, down, far = lax.optimization_barrier((part, stay, up, down, far))
        mine, other = [v.reshape(group, tokens, -1) for v in (part, to_core(part, 1))]
        pass_last(1)
        near = [v[i][k] for v in (up, down) for k in range(1, planes - 1) for i in range(2)]
        flow = [own[0], rest, own[0], rest] + near
        total = attend(rows, planes, mine, other, flow)
        last = jnp.where(plane == 0, planes - 1, 0)
        width = group * rows
        last_part = jnp.where(last * width // heads == core, mine, other)
        last_part = lax.dynamic_slice_in_dim(last_part, last * width % heads, width, 2)
        flow = [own[0], rest, *far] + near
        both = finish(rows, planes, total, last_part, gain, stay, flow)
        summed = both[0] + to_core(both[1], 1)
        span = local + 8
        projected = summed[:span]
        for s in range(1, group):
            projected = projected + to_member(summed[s * span : (s + 1) * span], s)
        stats = projected[local + 1 : local + 3, :local]
    else:
        pieces = [to_member(own[s], s) for s in members]
        down_plane = in_plane([to_member(down_own[s], s) for s in members])
        arrived = [to_member(context, s) for s in members]
        stay = [to_member(stay_own[s], s) for s in members]
        parts = [to_core(jnp.concatenate(arrived, axis=0), t) for t in cores]
        lines = [[p * group + m for p in range(planes)] for m in range(group)]
        chunk = jnp.zeros((group * rows, features), BF16)
        for s in members:
            chunk = lax.dynamic_update_slice_in_dim(chunk, pieces[s], (member ^ s) * rows, 0)
        weight = lax.all_gather(chunk, "wide", axis_index_groups=lines, tiled=True)
        all_down = lax.all_gather(down_plane, "wide", axis_index_groups=lines, tiled=True)

        def by_core(value):
            value = value.reshape(group, narrows, local, -1)
            return value.swapaxes(0, 1).reshape(group * tokens, -1)

        heads = context.shape[1]
        attn_sum = jnp.zeros((), F32)
        for t in cores:
            share = block(weight, core ^ t, heads, 0)
            attn_sum = attn_sum + jnp.dot(parts[t], share, preferred_element_type=F32)
        stream = (jnp.concatenate(stay, axis=0).astype(F32) + attn_sum).astype(BF16)
        stream = by_core(stream).astype(F32)
        scaled = (stream * gain.astype(F32)).astype(BF16).reshape(narrows, side_rows, features)
        gains = jnp.broadcast_to(gain[None], (narrows, 8, features))
        scaled = jnp.concatenate([scaled, gains], axis=1)
        stats = jnp.stack([jnp.sum(stream, axis=1), jnp.sum(stream * stream, axis=1)])
        stats_own = stats.reshape(2, narrows, group, local)

        def share_of_core(k):
            lhs = lax.dynamic_index_in_dim(scaled, k, 0, keepdims=False)
            return lax.dot_general(lhs, all_down, (((1,), (1,)), ((), ())), preferred_element_type=F32)

        summed = sum_cores(share_of_core)
        tail = summed[side_rows:]
        projected = sum_members(
            lambda s: jnp.concatenate([summed[s * local : (s + 1) * local], tail], axis=0)
        )
        summed_stats = sum_cores(lambda k: lax.dynamic_index_in_dim(stats_own, k, 1, keepdims=False))
        stats = sum_members(lambda s: summed_stats[:, s])
    projected, gain_map = projected[:local], projected[local]

    width = out_weight.shape[1] * narrows
    mean = stats[0] / width
    spread = stats[1] / width - mean * mean
    side_in = (projected - mean[:, None] * gain_map[None, :]) / jnp.sqrt(spread + 1e-06)[:, None]
    half = side_in.shape[1] // 2
    f_w, g_w = f_weight.astype(F32), g_weight.astype(F32)
    first, second = side_in[:, :half], side_in[:, half:]
    f_value, f_pull = jax.vjp(coupling, second, f_w)
    upper = first + f_value
    g_value, g_pull = jax.vjp(coupling, upper, g_w)
    lower = second + g_value
    side_out = jnp.concatenate([upper, lower], axis=1)
    misfit = (side_out - targets) / (local * wides * narrows)
    upper_back, g_local = g_pull(misfit[:, half:])
    f_local = f_pull(misfit[:, :half] + upper_back)[1]

    if (2 * half) % (wides * narrows * 8):
        f_total, g_total = lax.psum((f_local, g_local), ("wide", "narrow"))
        return side_out, f_total, g_total

    grads = jnp.concatenate([f_local, g_local], axis=0)
    share = 2 * half // narrows
    grads = sum_cores(lambda k: block(grads, k, share, 0))
    share = share // group
    part = grads
    grads = sum_members(lambda s: block(part, member ^ s, share, 0))
    share = share // planes

    def shift(value, k):
        return lax.ppermute(value, "wide", [(i, (i + k * group) % wides) for i in range(wides)])

    part = grads
    grads = block(part, plane, share, 0)
    for k in range(1, planes):
        grads = grads + shift(block(part, (plane + k) % planes, share, 0), k)
    whole = jnp.zeros((planes * share, half), F32)
    for k in range(planes):
        piece = shift(grads, k) if k else grads
        whole = lax.dynamic_update_slice_in_dim(whole, piece, (plane - k) % planes * share, 0)
    share = share * planes
    part, whole = whole, jnp.zeros((group * share, half), F32)
    for s in members:
        whole = lax.dynamic_update_slice_in_dim(whole, to_member(part, s), (member ^ s) * share, 0)
    share = share * group
    part, whole = whole, jnp.zeros((narrows * share, half), F32)
    for t in range(narrows):
        whole = lax.dynamic_update_slice_in_dim(whole, to_core(part, t), (core ^ t) * share, 0)
    return side_out, whole[:half], whole[half:]


def solution(mesh):
    wides, narrows = mesh.shape["wide"], mesh.shape["narrow"]
    group = GROUP if wides % GROUP == 0 else 1
    in_specs = (
        P("wide", "narrow"),
        P("wide", "narrow"),
        P("wide", "narrow"),
        P("narrow"),
        P("narrow", "wide"),
        P(),
        P(),
        P(("wide", "narrow"), None),
    )
    out_specs = (P(("wide", "narrow"), None), P(), P())
    return jax.shard_map(
        functools.partial(per_device, group, wides, narrows),
        mesh=mesh,
        in_specs=in_specs,
        out_specs=out_specs,
        check_vma=False,
    )
```

```python
import functools

import jax
import jax.numpy as jnp
from jax import lax
from jax.experimental import pallas as pl
from jax.experimental.pallas import tpu as pltpu
from jax.sharding import PartitionSpec as P

HIGH = lax.Precision.HIGH
F32 = jnp.float32
BF16 = jnp.bfloat16
GROUP = 4


def coupling(values, weight):
    return jax.nn.gelu(jnp.dot(values, weight, precision=HIGH))


def place():
    wide, core = lax.axis_index("wide"), lax.axis_index("narrow")
    return wide // GROUP, wide % GROUP, core


ROUTES = ((0, 1, 4, 5), (1, 0, 2, 3), (3, 2, 0, 1), (5, 4, 1, 0))
LAST = 5


def part_of(flow, at, p):
    return flow[2 * ROUTES[at][p] :][:2]


def share_of(pair, s, start, count, span):
    at = start + (s - 1) * span if s else start
    return pair[1 if s else 0].at[pl.ds(at, count)]


def attend_kernel(rows, planes, *refs):
    mine_ref, other_ref, *flow, out_ref, weight, sems = refs
    plane, member, core = place()
    span = flow[0].shape[0]

    for at in range(planes):

        @pl.when((pl.program_id(0) == 0) & (plane == at))
        def _():
            copies = []
            for p in range(planes):
                if ROUTES[at][p] == LAST:
                    weight[p * GROUP * rows : (p + 1) * GROUP * rows] = jnp.zeros((GROUP * rows, weight.shape[1]), BF16)
                    continue
                for s in range(GROUP):
                    target = pl.multiple_of((p * GROUP + (member ^ s)) * rows, 64)
                    source = share_of(part_of(flow, at, p), s, 0, rows, span)
                    copies.append(pltpu.make_async_copy(source, weight.at[pl.ds(target, rows)], sems.at[p, s]))
            for copy in copies:
                copy.start()
            for copy in copies:
                copy.wait()

    group, local, heads = mine_ref.shape
    for h in range(0, group, 2):
        lhs = mine_ref[h : h + 2].reshape(2 * local, heads)
        rhs = other_ref[h : h + 2].reshape(2 * local, heads)
        at = pl.multiple_of(core * heads, 128)
        total = jnp.dot(lhs, weight[pl.ds(at, heads)], preferred_element_type=F32)
        at = pl.multiple_of((1 - core) * heads, 128)
        total += jnp.dot(rhs, weight[pl.ds(at, heads)], preferred_element_type=F32)
        out_ref[h * local : (h + 2) * local] = total


def attend(rows, planes, mine, other, flow):
    group, tokens, heads = mine.shape
    count = flow[0].shape[1]
    part = pl.BlockSpec((group, tokens // 2, heads), lambda i: (0, i, 0))
    return pl.pallas_call(
        functools.partial(attend_kernel, rows, planes),
        grid=(2,),
        in_specs=[part, part] + [pl.BlockSpec(memory_space=pl.ANY)] * len(flow),
        out_specs=pl.BlockSpec((group * tokens // 2, count), lambda i: (i, 0)),
        out_shape=jax.ShapeDtypeStruct((group * tokens, count), F32),
        scratch_shapes=[pltpu.VMEM((2 * heads, count), BF16), pltpu.SemaphoreType.DMA((planes, group))],
        compiler_params=pltpu.CompilerParams(vmem_limit_bytes=40 << 20),
        cost_estimate=pl.CostEstimate(
            flops=4 * group * tokens * heads * count, bytes_accessed=16 << 20, transcendentals=0
        ),
    )(mine, other, *flow)


def finish_kernel(rows, planes, *refs):
    total_ref, far_ref, gain_ref, *refs = refs
    stay_refs, refs = refs[:GROUP], refs[GROUP:]
    *flow, keep_ref, send_ref, weight, down, scaled, sums, sems, down_sems = refs
    plane, member, core = place()
    span = flow[0].shape[0]
    columns = span - rows

    def far_copies():
        out = []
        for s in range(GROUP):
            target = pl.multiple_of((member ^ s) * rows, 64)
            source = share_of(flow[2 * LAST :], s, 0, rows, span)
            out.append(pltpu.make_async_copy(source, weight.at[pl.ds(target, rows)], sems.at[s]))
        return out

    def down_copies(at):
        out = []
        for p in range(planes):
            for s in range(GROUP):
                target = pl.multiple_of((p * GROUP + (member ^ s)) * columns, 16)
                source = share_of(part_of(flow, at, p), s, rows, columns, span)
                out.append(pltpu.make_async_copy(source, down.at[pl.ds(target, columns)], down_sems.at[p, s]))
        return out

    far = far_copies()
    for copy in far:
        copy.start()
    for at in range(planes):

        @pl.when(plane == at)
        def _():
            for copy in down_copies(at):
                copy.start()

    for copy in far:
        copy.wait()
    local = stay_refs[0].shape[0] // 2
    half = GROUP * local
    gain = gain_ref[...].astype(F32)
    for i in range(2):
        for h in range(0, GROUP, 2):
            at = i * half + h * local
            lhs = jnp.concatenate([far_ref[h + g, i * local : (i + 1) * local] for g in range(2)], axis=0)
            total = total_ref[at : at + 2 * local] + jnp.dot(lhs, weight[...], preferred_element_type=F32)
            stay = jnp.concatenate([stay_refs[h + g][i * local : (i + 1) * local] for g in range(2)], axis=0)
            stream = (stay.astype(F32) + total).astype(BF16).astype(F32)
            scaled[at : at + 2 * local] = (stream * gain).astype(BF16)
            row_sum = jnp.sum(stream, axis=1, keepdims=True)
            squares = jnp.sum(stream * stream, axis=1, keepdims=True)
            lane = lax.broadcasted_iota(jnp.int32, (2 * local, 128), 1)
            both = jnp.where(lane == 0, row_sum, jnp.where(lane == 1, squares, 0.0))
            sums[:, at : at + 2 * local] = both.T[:8]

    for at in range(planes):

        @pl.when(plane == at)
        def _():
            for copy in down_copies(at):
                copy.wait()

    dims = (((1,), (1,)), ((), ()))
    gains = jnp.broadcast_to(gain_ref[...], (16, gain_ref.shape[1]))
    gains = lax.dot_general(gains, down[...], dims, preferred_element_type=F32)
    line = local + 8
    for out_ref, k in ((send_ref, 1 - core), (keep_ref, core)):
        at = pl.multiple_of(k * half, 128)
        value = lax.dot_general(scaled[pl.ds(at, half)], down[...], dims, preferred_element_type=F32)
        stats = sums[:, pl.ds(at, half)]
        for s in range(GROUP):
            out_ref[s * line : s * line + local] = value[s * local : (s + 1) * local]
            out_ref[s * line + local : (s + 1) * line] = gains[:8]
            out_ref[s * line + local + 1 : s * line + local + 3, :local] = stats[:2, s * local : (s + 1) * local]


def finish(rows, planes, total, far, gain, stay, flow):
    count = total.shape[1]
    tokens = total.shape[0]
    span = flow[0].shape[0]
    out = (span - rows) * GROUP * planes
    inside = pl.BlockSpec(memory_space=pltpu.VMEM)
    return pl.pallas_call(
        functools.partial(finish_kernel, rows, planes),
        in_specs=[inside] * (3 + GROUP) + [pl.BlockSpec(memory_space=pl.ANY)] * len(flow),
        out_specs=[inside, inside],
        out_shape=[jax.ShapeDtypeStruct((tokens // 2 + 8 * GROUP, out), F32)] * 2,
        scratch_shapes=[
            pltpu.VMEM((GROUP * rows, count), BF16),
            pltpu.VMEM((out, count), BF16),
            pltpu.VMEM((tokens, count), BF16),
            pltpu.VMEM((8, tokens), F32),
            pltpu.SemaphoreType.DMA((GROUP,)),
            pltpu.SemaphoreType.DMA((planes, GROUP)),
        ],
        compiler_params=pltpu.CompilerParams(vmem_limit_bytes=40 << 20),
        cost_estimate=pl.CostEstimate(
            flops=2 * tokens * count * (GROUP * rows + out), bytes_accessed=16 << 20, transcendentals=0
        ),
    )(total, far, gain, *stay, *flow)


def per_device(group, wides, narrows, context, out_weight, residual, ln_gain, side_down, f_weight, g_weight, targets):
    planes = wides // group
    wide, core = lax.axis_index("wide"), lax.axis_index("narrow")
    plane, member = wide // group, wide % group
    short = group == GROUP and planes == 4 and narrows == 2
    features = out_weight.shape[1] // group
    rows = out_weight.shape[0]
    tokens = context.shape[0]
    local = tokens // narrows
    members = range(group)
    cores = range(narrows)

    def to_member(value, s):
        pairs = [(i, i - i % group + (i % group ^ s)) for i in range(wides)]
        return lax.ppermute(value, "wide", pairs) if s else value

    def to_core(value, t):
        return lax.ppermute(value, "narrow", [(i, i ^ t) for i in range(narrows)]) if t else value

    def block(value, index, size, axis):
        return lax.dynamic_slice_in_dim(value, index * size, size, axis)

    def sum_cores(pick):
        total = pick(core)
        for t in range(1, narrows):
            total = total + to_core(pick(core ^ t), t)
        return total

    def sum_members(pick):
        total = pick(0)
        for s in range(1, group):
            total = total + to_member(pick(s), s)
        return total

    own = [block(out_weight, member ^ s, features, 1) for s in members]
    down_own = [block(side_down.T, member ^ s, features, 1) for s in members]
    stay_own = [block(residual, member ^ s, features, 1) for s in members]
    gain = block(ln_gain, member, features, 0)[None, :]
    columns = down_own[0].shape[0]
    side_rows = group * local

    def in_plane(downs):
        value = jnp.zeros((group * columns, features), BF16)
        for s in members:
            value = lax.dynamic_update_slice_in_dim(value, downs[s], (member ^ s) * columns, 0)
        return value

    if short:
        own = [jnp.concatenate(pair, axis=0) for pair in zip(own, down_own)]
        boxes = [jnp.concatenate([context, value], axis=1) for value in stay_own[1:]]

        def line(value, pairs):
            pairs = [(i * group + m, j * group + m) for i, j in pairs for m in members]
            return lax.ppermute(value, "wide", pairs)

        outward, inward = [(1, 0), (2, 3)], [(1, 2), (2, 1)]

        def step_one(value):
            return line(value, outward + [(0, 1), (3, 2)]), line(value, inward)

        def step_two(first, second):
            return line(first, inward), line(second, outward)

        own_one = step_one(own[0])
        own_two = step_two(*own_one)
        rest = jnp.concatenate([to_member(own[s], s) for s in range(1, group)], axis=0)

        rest, boxes, own_two = lax.optimization_barrier((rest, boxes, own_two))
        rest_one = step_one(rest)
        own_last = line(own_two[0], outward)
        arrived = [to_member(boxes[0], 1), to_member(boxes[1], 2)]

        arrived, boxes, rest_one, own_last = lax.optimization_barrier((arrived, boxes, rest_one, own_last))
        rest_two = step_two(*rest_one)
        arrived.append(to_member(boxes[2], 3))

        arrived, rest_two = lax.optimization_barrier((arrived, rest_two))
        rest_last = line(rest_two[0], outward)
        heads = context.shape[1]
        part = jnp.concatenate([context] + [v[:, :heads] for v in arrived], axis=0)
        stay = stay_own[:1] + [v[:, heads:] for v in arrived]
        mine, other = [v.reshape(group, tokens, -1) for v in (part, to_core(part, 1))]
        flow = [own[0], rest]
        for pair in zip(own_one + own_two, rest_one + rest_two):
            flow += pair
        total = attend(rows, planes, mine, other, flow)
        last = jnp.where(plane == 0, planes - 1, 0)
        width = group * rows
        last_part = jnp.where(last * width // heads == core, mine, other)
        last_part = lax.dynamic_slice_in_dim(last_part, last * width % heads, width, 2)
        flow += [own_last, rest_last]
        keep, send = finish(rows, planes, total, last_part, gain, stay, flow)
        summed = keep + to_core(send, 1)
        span = local + 8
        projected = summed[:span]
        for s in range(1, group):
            projected = projected + to_member(summed[s * span : (s + 1) * span], s)
        stats = projected[local + 1 : local + 3, :local]
    else:
        pieces = [to_member(own[s], s) for s in members]
        down_plane = in_plane([to_member(down_own[s], s) for s in members])
        arrived = [to_member(context, s) for s in members]
        stay = [to_member(stay_own[s], s) for s in members]
        parts = [to_core(jnp.concatenate(arrived, axis=0), t) for t in cores]
        lines = [[p * group + m for p in range(planes)] for m in range(group)]
        chunk = jnp.zeros((group * rows, features), BF16)
        for s in members:
            chunk = lax.dynamic_update_slice_in_dim(chunk, pieces[s], (member ^ s) * rows, 0)
        weight = lax.all_gather(chunk, "wide", axis_index_groups=lines, tiled=True)
        all_down = lax.all_gather(down_plane, "wide", axis_index_groups=lines, tiled=True)

        def by_core(value):
            value = value.reshape(group, narrows, local, -1)
            return value.swapaxes(0, 1).reshape(group * tokens, -1)

        heads = context.shape[1]
        attn_sum = jnp.zeros((), F32)
        for t in cores:
            share = block(weight, core ^ t, heads, 0)
            attn_sum = attn_sum + jnp.dot(parts[t], share, preferred_element_type=F32)
        stream = (jnp.concatenate(stay, axis=0).astype(F32) + attn_sum).astype(BF16)
        stream = by_core(stream).astype(F32)
        scaled = (stream * gain.astype(F32)).astype(BF16).reshape(narrows, side_rows, features)
        gains = jnp.broadcast_to(gain[None], (narrows, 8, features))
        scaled = jnp.concatenate([scaled, gains], axis=1)
        stats = jnp.stack([jnp.sum(stream, axis=1), jnp.sum(stream * stream, axis=1)])
        stats_own = stats.reshape(2, narrows, group, local)

        def share_of_core(k):
            lhs = lax.dynamic_index_in_dim(scaled, k, 0, keepdims=False)
            return lax.dot_general(lhs, all_down, (((1,), (1,)), ((), ())), preferred_element_type=F32)

        summed = sum_cores(share_of_core)
        tail = summed[side_rows:]
        projected = sum_members(
            lambda s: jnp.concatenate([summed[s * local : (s + 1) * local], tail], axis=0)
        )
        summed_stats = sum_cores(lambda k: lax.dynamic_index_in_dim(stats_own, k, 1, keepdims=False))
        stats = sum_members(lambda s: summed_stats[:, s])
    projected, gain_map = projected[:local], projected[local]

    width = out_weight.shape[1] * narrows
    mean = stats[0] / width
    spread = stats[1] / width - mean * mean
    side_in = (projected - mean[:, None] * gain_map[None, :]) / jnp.sqrt(spread + 1e-06)[:, None]
    half = side_in.shape[1] // 2
    f_w, g_w = f_weight.astype(F32), g_weight.astype(F32)
    first, second = side_in[:, :half], side_in[:, half:]
    f_value, f_pull = jax.vjp(coupling, second, f_w)
    upper = first + f_value
    g_value, g_pull = jax.vjp(coupling, upper, g_w)
    lower = second + g_value
    side_out = jnp.concatenate([upper, lower], axis=1)
    misfit = (side_out - targets) / (local * wides * narrows)
    upper_back, g_local = g_pull(misfit[:, half:])
    f_local = f_pull(misfit[:, :half] + upper_back)[1]

    if (2 * half) % (wides * narrows * 8):
        f_total, g_total = lax.psum((f_local, g_local), ("wide", "narrow"))
        return side_out, f_total, g_total

    grads = jnp.concatenate([f_local, g_local], axis=0)
    share = 2 * half // narrows
    grads = sum_cores(lambda k: block(grads, k, share, 0))
    share = share // group
    part = grads
    grads = sum_members(lambda s: block(part, member ^ s, share, 0))
    share = share // planes

    def shift(value, k):
        return lax.ppermute(value, "wide", [(i, (i + k * group) % wides) for i in range(wides)])

    part = grads
    grads = block(part, plane, share, 0)
    for k in range(1, planes):
        grads = grads + shift(block(part, (plane + k) % planes, share, 0), k)
    whole = jnp.zeros((planes * share, half), F32)
    for k in range(planes):
        piece = shift(grads, k) if k else grads
        whole = lax.dynamic_update_slice_in_dim(whole, piece, (plane - k) % planes * share, 0)
    share = share * planes
    part, whole = whole, jnp.zeros((group * share, half), F32)
    for s in members:
        whole = lax.dynamic_update_slice_in_dim(whole, to_member(part, s), (member ^ s) * share, 0)
    share = share * group
    part, whole = whole, jnp.zeros((narrows * share, half), F32)
    for t in range(narrows):
        whole = lax.dynamic_update_slice_in_dim(whole, to_core(part, t), (core ^ t) * share, 0)
    return side_out, whole[:half], whole[half:]


def solution(mesh):
    wides, narrows = mesh.shape["wide"], mesh.shape["narrow"]
    group = GROUP if wides % GROUP == 0 else 1
    in_specs = (
        P("wide", "narrow"),
        P("wide", "narrow"),
        P("wide", "narrow"),
        P("narrow"),
        P("narrow", "wide"),
        P(),
        P(),
        P(("wide", "narrow"), None),
    )
    out_specs = (P(("wide", "narrow"), None), P(), P())
    return jax.shard_map(
        functools.partial(per_device, group, wides, narrows),
        mesh=mesh,
        in_specs=in_specs,
        out_specs=out_specs,
        check_vma=False,
    )
```

```python
import functools

import jax
import jax.numpy as jnp
from jax import lax
from jax.experimental import pallas as pl
from jax.experimental.pallas import tpu as pltpu
from jax.sharding import PartitionSpec as P

HIGH = lax.Precision.HIGH
F32 = jnp.float32
BF16 = jnp.bfloat16
GROUP = 4


def coupling(values, weight):
    return jax.nn.gelu(jnp.dot(values, weight, precision=HIGH))


def place():
    wide, core = lax.axis_index("wide"), lax.axis_index("narrow")
    return wide // GROUP, wide % GROUP, core


ROUTES = ((0, 1, 4, 5), (1, 0, 2, 3), (3, 2, 0, 1), (5, 4, 1, 0))
LAST = 5


def part_of(flow, at, p):
    return flow[2 * ROUTES[at][p] :][:2]


def share_of(pair, s, start, count, span):
    at = start + (s - 1) * span if s else start
    return pair[1 if s else 0].at[pl.ds(at, count)]


def attend_kernel(rows, planes, *refs):
    mine_ref, other_ref, *refs = refs
    stay_refs, (*flow, out_ref, weight, sems) = refs[:GROUP], refs[GROUP:]
    plane, member, core = place()
    span = flow[0].shape[0]

    for at in range(planes):

        @pl.when((pl.program_id(0) == 0) & (plane == at))
        def _():
            copies = []
            for p in range(planes):
                if ROUTES[at][p] == LAST:
                    weight[p * GROUP * rows : (p + 1) * GROUP * rows] = jnp.zeros((GROUP * rows, weight.shape[1]), BF16)
                    continue
                for s in range(GROUP):
                    target = pl.multiple_of((p * GROUP + (member ^ s)) * rows, 64)
                    source = share_of(part_of(flow, at, p), s, 0, rows, span)
                    copies.append(pltpu.make_async_copy(source, weight.at[pl.ds(target, rows)], sems.at[p, s]))
            for copy in copies:
                copy.start()
            for copy in copies:
                copy.wait()

    group, local, heads = mine_ref.shape
    for h in range(0, group, 2):
        lhs = mine_ref[h : h + 2].reshape(2 * local, heads)
        rhs = other_ref[h : h + 2].reshape(2 * local, heads)
        at = pl.multiple_of(core * heads, 128)
        total = jnp.dot(lhs, weight[pl.ds(at, heads)], preferred_element_type=F32)
        at = pl.multiple_of((1 - core) * heads, 128)
        total += jnp.dot(rhs, weight[pl.ds(at, heads)], preferred_element_type=F32)
        for g in range(2):
            stay = stay_refs[h + g][...].astype(F32)
            out_ref[(h + g) * local : (h + g + 1) * local] = stay + total[g * local : (g + 1) * local]


def attend(rows, planes, mine, other, stay, flow):
    group, tokens, heads = mine.shape
    count = flow[0].shape[1]
    part = pl.BlockSpec((group, tokens // 2, heads), lambda i: (0, i, 0))
    return pl.pallas_call(
        functools.partial(attend_kernel, rows, planes),
        grid=(2,),
        in_specs=[part, part]
        + [pl.BlockSpec((tokens // 2, count), lambda i: (i, 0))] * group
        + [pl.BlockSpec(memory_space=pl.ANY)] * len(flow),
        out_specs=pl.BlockSpec((group * tokens // 2, count), lambda i: (i, 0)),
        out_shape=jax.ShapeDtypeStruct((group * tokens, count), F32),
        scratch_shapes=[pltpu.VMEM((2 * heads, count), BF16), pltpu.SemaphoreType.DMA((planes, group))],
        compiler_params=pltpu.CompilerParams(vmem_limit_bytes=40 << 20),
        cost_estimate=pl.CostEstimate(
            flops=4 * group * tokens * heads * count, bytes_accessed=16 << 20, transcendentals=0
        ),
    )(mine, other, *stay, *flow)


def finish_kernel(rows, planes, *refs):
    total_ref, far_ref, gain_ref, *flow, keep_ref, send_ref, weight, down, sems, down_sems = refs
    plane, member, core = place()
    span = flow[0].shape[0]
    columns = span - rows

    def far_copies():
        out = []
        for s in range(GROUP):
            target = pl.multiple_of((member ^ s) * rows, 64)
            source = share_of(flow[2 * LAST :], s, 0, rows, span)
            out.append(pltpu.make_async_copy(source, weight.at[pl.ds(target, rows)], sems.at[s]))
        return out

    def down_copies(at):
        out = []
        for p in range(planes):
            for s in range(GROUP):
                target = pl.multiple_of((p * GROUP + (member ^ s)) * columns, 16)
                source = share_of(part_of(flow, at, p), s, rows, columns, span)
                out.append(pltpu.make_async_copy(source, down.at[pl.ds(target, columns)], down_sems.at[p, s]))
        return out

    far = far_copies()
    for copy in far:
        copy.start()
    for at in range(planes):

        @pl.when(plane == at)
        def _():
            for copy in down_copies(at):
                copy.start()

    for copy in far:
        copy.wait()
    gain = gain_ref[...].astype(F32)
    half = total_ref.shape[0] // 2
    local = half // GROUP
    line = local + 8
    dims = (((1,), (1,)), ((), ()))
    gains = None
    for out_ref, k in ((send_ref, 1 - core), (keep_ref, core)):
        for h in range(0, GROUP, 2):
            own_rows = pl.ds(pl.multiple_of(k * half + h * local, 128), 2 * local)
            total = total_ref[own_rows] + jnp.dot(far_ref[own_rows], weight[...], preferred_element_type=F32)
            stream = total.astype(BF16).astype(F32)
            row_sum = jnp.sum(stream, axis=1, keepdims=True)
            squares = jnp.sum(stream * stream, axis=1, keepdims=True)
            lane = lax.broadcasted_iota(jnp.int32, (2 * local, 128), 1)
            both = jnp.where(lane == 0, row_sum, jnp.where(lane == 1, squares, 0.0)).T
            if gains is None:
                for at in range(planes):

                    @pl.when(plane == at)
                    def _():
                        for copy in down_copies(at):
                            copy.wait()

                gains = jnp.broadcast_to(gain_ref[...], (16, gain_ref.shape[1]))
                gains = lax.dot_general(gains, down[...], dims, preferred_element_type=F32)[:8]
            scaled = (stream * gain).astype(BF16)
            value = lax.dot_general(scaled, down[...], dims, preferred_element_type=F32)
            for g in range(2):
                at = (h + g) * line
                out_ref[at : at + local] = value[g * local : (g + 1) * local]
                out_ref[at + local : at + line] = gains
                out_ref[at + local + 1 : at + local + 3, :local] = both[:2, g * local : (g + 1) * local]


def finish(rows, planes, total, far, gain, flow):
    count = total.shape[1]
    tokens = total.shape[0]
    span = flow[0].shape[0]
    out = (span - rows) * GROUP * planes
    inside = pl.BlockSpec(memory_space=pltpu.VMEM)
    return pl.pallas_call(
        functools.partial(finish_kernel, rows, planes),
        in_specs=[inside] * 3 + [pl.BlockSpec(memory_space=pl.ANY)] * len(flow),
        out_specs=[inside, inside],
        out_shape=[jax.ShapeDtypeStruct((tokens // 2 + 8 * GROUP, out), F32)] * 2,
        scratch_shapes=[
            pltpu.VMEM((GROUP * rows, count), BF16),
            pltpu.VMEM((out, count), BF16),
            pltpu.SemaphoreType.DMA((GROUP,)),
            pltpu.SemaphoreType.DMA((planes, GROUP)),
        ],
        compiler_params=pltpu.CompilerParams(vmem_limit_bytes=40 << 20),
        cost_estimate=pl.CostEstimate(
            flops=2 * tokens * count * (GROUP * rows + out), bytes_accessed=16 << 20, transcendentals=0
        ),
    )(total, far, gain, *flow)


def split(value):
    high = value.astype(BF16)
    return high, (value - high.astype(F32)).astype(BF16)


def times(value, weight, turned=False):
    count = value.shape[0]
    dims = (((1,), (1 if turned else 0,)), ((), ()))
    both = lax.dot_general(jnp.concatenate(split(value), axis=0), weight, dims, preferred_element_type=F32)
    return both[:count] + both[count:]


def outer(left, right):
    (left, left_low), (right, right_low) = split(left), split(right)
    left = jnp.concatenate([left, left, left_low], axis=0)
    right = jnp.concatenate([right, right_low, right], axis=0)
    return lax.dot_general(left, right, (((0,), (0,)), ((), ())), preferred_element_type=F32)


def gelu_and_slope(v):
    scale = 0.7978845608028654
    t = jnp.tanh(scale * (v + 0.044715 * (v * v * v)))
    slope = 0.5 * (1.0 + t) + 0.5 * v * (1.0 - t * t) * (scale * (1.0 + 3.0 * 0.044715 * (v * v)))
    return 0.5 * v * (1.0 + t), slope


def side_kernel(width, all_tokens, *refs):
    *part_refs, f_ref, g_ref, target_ref, out_ref, keep_ref, send_ref = refs
    local, features = out_ref.shape
    half = features // 2
    total = part_refs[0][...]
    for ref in part_refs[1:]:
        total = total + ref[...]
    tail = total[local:]
    stats = jnp.concatenate([tail[:, :local]] * (local // 8), axis=0).T
    mean = stats[:, 1:2] / width
    spread = stats[:, 2:3] / width - mean * mean
    side_in = (total[:local] - mean * tail[:1]) / jnp.sqrt(spread + 1e-06)
    first, second = side_in[:, :half], side_in[:, half:]
    f_w, g_w = f_ref[...], g_ref[...]
    f_value, f_slope = gelu_and_slope(times(second, f_w))
    upper = first + f_value
    g_value, g_slope = gelu_and_slope(times(upper, g_w))
    lower = second + g_value
    out_ref[:, :half] = upper
    out_ref[:, half:] = lower
    g_back = (lower - target_ref[:, half:]) / all_tokens * g_slope
    upper_back = (upper - target_ref[:, :half]) / all_tokens + times(g_back, g_w, turned=True)
    g_grad = outer(upper, g_back)
    f_grad = outer(second, upper_back * f_slope)
    core = lax.axis_index("narrow")

    @pl.when(core == 0)
    def _():
        keep_ref[...] = f_grad
        send_ref[...] = g_grad

    @pl.when(core != 0)
    def _():
        keep_ref[...] = g_grad
        send_ref[...] = f_grad


def side_block(width, all_tokens, parts, f_weight, g_weight, targets):
    inside = pl.BlockSpec(memory_space=pltpu.VMEM)
    grad = jax.ShapeDtypeStruct(f_weight.shape, F32)
    work = targets.shape[0] * f_weight.size
    return pl.pallas_call(
        functools.partial(side_kernel, width, all_tokens),
        in_specs=[inside] * (len(parts) + 3),
        out_specs=[inside] * 3,
        out_shape=[jax.ShapeDtypeStruct(targets.shape, F32), grad, grad],
        compiler_params=pltpu.CompilerParams(vmem_limit_bytes=24 << 20),
        cost_estimate=pl.CostEstimate(flops=24 * work, bytes_accessed=5 << 20, transcendentals=2 * targets.size),
    )(*parts, f_weight, g_weight, targets)


def per_device(group, wides, narrows, context, out_weight, residual, ln_gain, side_down, f_weight, g_weight, targets):
    planes = wides // group
    wide, core = lax.axis_index("wide"), lax.axis_index("narrow")
    plane, member = wide // group, wide % group
    short = group == GROUP and planes == 4 and narrows == 2
    features = out_weight.shape[1] // group
    rows = out_weight.shape[0]
    tokens = context.shape[0]
    local = tokens // narrows
    members = range(group)
    cores = range(narrows)

    def to_member(value, s):
        pairs = [(i, i - i % group + (i % group ^ s)) for i in range(wides)]
        return lax.ppermute(value, "wide", pairs) if s else value

    def to_core(value, t):
        return lax.ppermute(value, "narrow", [(i, i ^ t) for i in range(narrows)]) if t else value

    def block(value, index, size, axis):
        return lax.dynamic_slice_in_dim(value, index * size, size, axis)

    def sum_cores(pick):
        total = pick(core)
        for t in range(1, narrows):
            total = total + to_core(pick(core ^ t), t)
        return total

    def sum_members(pick):
        total = pick(0)
        for s in range(1, group):
            total = total + to_member(pick(s), s)
        return total

    own = [block(out_weight, member ^ s, features, 1) for s in members]
    down_own = [block(side_down.T, member ^ s, features, 1) for s in members]
    stay_own = [block(residual, member ^ s, features, 1) for s in members]
    gain = block(ln_gain, member, features, 0)[None, :]
    columns = down_own[0].shape[0]
    side_rows = group * local

    def in_plane(downs):
        value = jnp.zeros((group * columns, features), BF16)
        for s in members:
            value = lax.dynamic_update_slice_in_dim(value, downs[s], (member ^ s) * columns, 0)
        return value

    if short:
        own = [jnp.concatenate(pair, axis=0) for pair in zip(own, down_own)]
        boxes = [jnp.concatenate([context, value], axis=1) for value in stay_own[1:]]

        def line(value, pairs):
            pairs = [(i * group + m, j * group + m) for i, j in pairs for m in members]
            return lax.ppermute(value, "wide", pairs)

        outward, inward = [(1, 0), (2, 3)], [(1, 2), (2, 1)]

        def step_one(value):
            return line(value, outward + [(0, 1), (3, 2)]), line(value, inward)

        def step_two(first, second):
            return line(first, inward), line(second, outward)

        own_one = step_one(own[0])
        own_two = step_two(*own_one)
        rest = jnp.concatenate([to_member(own[s], s) for s in range(1, group)], axis=0)

        rest, boxes, own_two = lax.optimization_barrier((rest, boxes, own_two))
        rest_one = step_one(rest)
        own_last = line(own_two[0], outward)
        arrived = [to_member(boxes[0], 1), to_member(boxes[1], 2)]

        arrived, boxes, rest_one, own_last = lax.optimization_barrier((arrived, boxes, rest_one, own_last))
        rest_two = step_two(*rest_one)
        arrived.append(to_member(boxes[2], 3))

        arrived, rest_two = lax.optimization_barrier((arrived, rest_two))
        rest_last = line(rest_two[0], outward)
        heads = context.shape[1]
        part = jnp.concatenate([context] + [v[:, :heads] for v in arrived], axis=0)
        stay = stay_own[:1] + [v[:, heads:] for v in arrived]
        mine, other = [v.reshape(group, tokens, -1) for v in (part, to_core(part, 1))]
        flow = [own[0], rest]
        for pair in zip(own_one + own_two, rest_one + rest_two):
            flow += pair
        total = attend(rows, planes, mine, other, stay, flow)
        last = jnp.where(plane == 0, planes - 1, 0)
        width = group * rows
        last_part = jnp.where(last * width // heads == core, mine, other)
        last_part = lax.dynamic_slice_in_dim(last_part, last * width % heads, width, 2)
        last_part = last_part.reshape(group, narrows, local, width).swapaxes(0, 1).reshape(-1, width)
        flow += [own_last, rest_last]
        keep, send = finish(rows, planes, total, last_part, gain, flow)
        summed = keep + to_core(send, 1)
        span = local + 8
        pieces = [summed[:span]]
        pieces += [to_member(summed[s * span : (s + 1) * span], s) for s in range(1, group)]
        width = out_weight.shape[1] * narrows
        all_tokens = local * wides * narrows
        side_out, keep, send = side_block(width, all_tokens, pieces, f_weight, g_weight, targets)
        grads = keep + to_core(send, 1)
    else:
        pieces = [to_member(own[s], s) for s in members]
        down_plane = in_plane([to_member(down_own[s], s) for s in members])
        arrived = [to_member(context, s) for s in members]
        stay = [to_member(stay_own[s], s) for s in members]
        parts = [to_core(jnp.concatenate(arrived, axis=0), t) for t in cores]
        lines = [[p * group + m for p in range(planes)] for m in range(group)]
        chunk = jnp.zeros((group * rows, features), BF16)
        for s in members:
            chunk = lax.dynamic_update_slice_in_dim(chunk, pieces[s], (member ^ s) * rows, 0)
        weight = lax.all_gather(chunk, "wide", axis_index_groups=lines, tiled=True)
        all_down = lax.all_gather(down_plane, "wide", axis_index_groups=lines, tiled=True)

        def by_core(value):
            value = value.reshape(group, narrows, local, -1)
            return value.swapaxes(0, 1).reshape(group * tokens, -1)

        heads = context.shape[1]
        attn_sum = jnp.zeros((), F32)
        for t in cores:
            share = block(weight, core ^ t, heads, 0)
            attn_sum = attn_sum + jnp.dot(parts[t], share, preferred_element_type=F32)
        stream = (jnp.concatenate(stay, axis=0).astype(F32) + attn_sum).astype(BF16)
        stream = by_core(stream).astype(F32)
        scaled = (stream * gain.astype(F32)).astype(BF16).reshape(narrows, side_rows, features)
        gains = jnp.broadcast_to(gain[None], (narrows, 8, features))
        scaled = jnp.concatenate([scaled, gains], axis=1)
        stats = jnp.stack([jnp.sum(stream, axis=1), jnp.sum(stream * stream, axis=1)])
        stats_own = stats.reshape(2, narrows, group, local)

        def share_of_core(k):
            lhs = lax.dynamic_index_in_dim(scaled, k, 0, keepdims=False)
            return lax.dot_general(lhs, all_down, (((1,), (1,)), ((), ())), preferred_element_type=F32)

        summed = sum_cores(share_of_core)
        tail = summed[side_rows:]
        projected = sum_members(
            lambda s: jnp.concatenate([summed[s * local : (s + 1) * local], tail], axis=0)
        )
        summed_stats = sum_cores(lambda k: lax.dynamic_index_in_dim(stats_own, k, 1, keepdims=False))
        stats = sum_members(lambda s: summed_stats[:, s])
        projected, gain_map = projected[:local], projected[local]

        width = out_weight.shape[1] * narrows
        mean = stats[0] / width
        spread = stats[1] / width - mean * mean
        side_in = (projected - mean[:, None] * gain_map[None, :]) / jnp.sqrt(spread + 1e-06)[:, None]
        half = side_in.shape[1] // 2
        f_w, g_w = f_weight.astype(F32), g_weight.astype(F32)
        first, second = side_in[:, :half], side_in[:, half:]
        f_value, f_pull = jax.vjp(coupling, second, f_w)
        upper = first + f_value
        g_value, g_pull = jax.vjp(coupling, upper, g_w)
        lower = second + g_value
        side_out = jnp.concatenate([upper, lower], axis=1)
        misfit = (side_out - targets) / (local * wides * narrows)
        upper_back, g_local = g_pull(misfit[:, half:])
        f_local = f_pull(misfit[:, :half] + upper_back)[1]
        f_total, g_total = lax.psum((f_local, g_local), ("wide", "narrow"))
        return side_out, f_total, g_total

    half = grads.shape[1]
    share = grads.shape[0] // group
    part = grads
    grads = sum_members(lambda s: block(part, member ^ s, share, 0))
    share = share // planes

    def shift(value, k):
        return lax.ppermute(value, "wide", [(i, (i + k * group) % wides) for i in range(wides)])

    part = grads
    grads = block(part, plane, share, 0)
    for k in range(1, planes):
        grads = grads + shift(block(part, (plane + k) % planes, share, 0), k)
    whole = jnp.zeros((planes * share, half), F32)
    for k in range(planes):
        piece = shift(grads, k) if k else grads
        whole = lax.dynamic_update_slice_in_dim(whole, piece, (plane - k) % planes * share, 0)
    share = share * planes
    part, whole = whole, jnp.zeros((group * share, half), F32)
    for s in members:
        whole = lax.dynamic_update_slice_in_dim(whole, to_member(part, s), (member ^ s) * share, 0)
    other = to_core(whole, 1)
    return side_out, jnp.where(core == 0, whole, other), jnp.where(core == 0, other, whole)


def solution(mesh):
    wides, narrows = mesh.shape["wide"], mesh.shape["narrow"]
    group = GROUP if wides % GROUP == 0 else 1
    in_specs = (
        P("wide", "narrow"),
        P("wide", "narrow"),
        P("wide", "narrow"),
        P("narrow"),
        P("narrow", "wide"),
        P(),
        P(),
        P(("wide", "narrow"), None),
    )
    out_specs = (P(("wide", "narrow"), None), P(), P())
    return jax.shard_map(
        functools.partial(per_device, group, wides, narrows),
        mesh=mesh,
        in_specs=in_specs,
        out_specs=out_specs,
        check_vma=False,
    )
```

```python
import functools

import jax
import jax.numpy as jnp
from jax import lax
from jax.experimental import pallas as pl
from jax.experimental.pallas import tpu as pltpu
from jax.sharding import PartitionSpec as P

HIGH = lax.Precision.HIGH
F32 = jnp.float32
BF16 = jnp.bfloat16
GROUP = 4


def coupling(values, weight):
    return jax.nn.gelu(jnp.dot(values, weight, precision=HIGH))


def place():
    wide, core = lax.axis_index("wide"), lax.axis_index("narrow")
    return wide // GROUP, wide % GROUP, core


ROUTES = ((0, 1, 4, 5), (1, 0, 2, 3), (3, 2, 0, 1), (5, 4, 1, 0))
LAST = 5


def part_of(flow, at, p):
    return flow[2 * ROUTES[at][p] :][:2]


def share_of(pair, s, start, count, span):
    at = start + (s - 1) * span if s else start
    return pair[1 if s else 0].at[pl.ds(at, count)]


def attend_kernel(rows, planes, *refs):
    mine_ref, other_ref, *refs = refs
    stay_refs, (*flow, out_ref, down_ref, weight, sems, down_sems) = refs[:GROUP], refs[GROUP:]
    plane, member, core = place()
    span = flow[0].shape[0]
    columns = span - rows

    for at in range(planes):

        @pl.when((pl.program_id(0) == 0) & (plane == at))
        def _():
            copies = []
            for p in range(planes):
                if ROUTES[at][p] == LAST:
                    weight[p * GROUP * rows : (p + 1) * GROUP * rows] = jnp.zeros((GROUP * rows, weight.shape[1]), BF16)
                    ends = (p * GROUP * columns, (p + 1) * GROUP * columns)
                    down_ref[ends[0] : ends[1]] = jnp.zeros((GROUP * columns, weight.shape[1]), BF16)
                    continue
                for s in range(GROUP):
                    target = pl.multiple_of((p * GROUP + (member ^ s)) * rows, 64)
                    source = share_of(part_of(flow, at, p), s, 0, rows, span)
                    copies.append(pltpu.make_async_copy(source, weight.at[pl.ds(target, rows)], sems.at[p, s]))
                    target = pl.multiple_of((p * GROUP + (member ^ s)) * columns, 16)
                    source = share_of(part_of(flow, at, p), s, rows, columns, span)
                    target = down_ref.at[pl.ds(target, columns)]
                    copies.append(pltpu.make_async_copy(source, target, down_sems.at[p, s]))
            for copy in copies:
                copy.start()
            for copy in copies:
                copy.wait()

    group, local, heads = mine_ref.shape
    for h in range(0, group, 2):
        lhs = mine_ref[h : h + 2].reshape(2 * local, heads)
        rhs = other_ref[h : h + 2].reshape(2 * local, heads)
        at = pl.multiple_of(core * heads, 128)
        total = jnp.dot(lhs, weight[pl.ds(at, heads)], preferred_element_type=F32)
        at = pl.multiple_of((1 - core) * heads, 128)
        total += jnp.dot(rhs, weight[pl.ds(at, heads)], preferred_element_type=F32)
        for g in range(2):
            stay = stay_refs[h + g][...].astype(F32)
            out_ref[(h + g) * local : (h + g + 1) * local] = stay + total[g * local : (g + 1) * local]


def attend(rows, planes, mine, other, stay, flow):
    group, tokens, heads = mine.shape
    count = flow[0].shape[1]
    part = pl.BlockSpec((group, tokens // 2, heads), lambda i: (0, i, 0))
    out = (flow[0].shape[0] - rows) * group * planes
    return pl.pallas_call(
        functools.partial(attend_kernel, rows, planes),
        grid=(2,),
        in_specs=[part, part]
        + [pl.BlockSpec((tokens // 2, count), lambda i: (i, 0))] * group
        + [pl.BlockSpec(memory_space=pl.ANY)] * len(flow),
        out_specs=[
            pl.BlockSpec((group * tokens // 2, count), lambda i: (i, 0)),
            pl.BlockSpec((out, count), lambda i: (0, 0)),
        ],
        out_shape=[
            jax.ShapeDtypeStruct((group * tokens, count), F32),
            jax.ShapeDtypeStruct((out, count), BF16),
        ],
        scratch_shapes=[
            pltpu.VMEM((2 * heads, count), BF16),
            pltpu.SemaphoreType.DMA((planes, group)),
            pltpu.SemaphoreType.DMA((planes, group)),
        ],
        compiler_params=pltpu.CompilerParams(vmem_limit_bytes=28 << 20),
        cost_estimate=pl.CostEstimate(
            flops=4 * group * tokens * heads * count, bytes_accessed=16 << 20, transcendentals=0
        ),
    )(mine, other, *stay, *flow)


def finish_kernel(rows, planes, *refs):
    total_ref, far_ref, gain_ref, near_ref, *flow, keep_ref, send_ref, weight, down, sems, down_sems, near_sem = refs
    plane, member, core = place()
    span = flow[0].shape[0]
    columns = span - rows

    def far_copies():
        out = []
        for s in range(GROUP):
            target = pl.multiple_of((member ^ s) * rows, 64)
            source = share_of(flow, s, 0, rows, span)
            out.append(pltpu.make_async_copy(source, weight.at[pl.ds(target, rows)], sems.at[s]))
        return out

    def down_copies(p):
        out = []
        for s in range(GROUP):
            target = pl.multiple_of((p * GROUP + (member ^ s)) * columns, 16)
            source = share_of(flow, s, rows, columns, span)
            out.append(pltpu.make_async_copy(source, down.at[pl.ds(target, columns)], down_sems.at[s]))
        return out

    near = pltpu.make_async_copy(near_ref, down, near_sem)
    near.start()
    far = far_copies()
    for copy in far:
        copy.start()
    near.wait()
    ends = [(at, ROUTES[at].index(LAST)) for at in range(planes) if LAST in ROUTES[at]]
    for at, p in ends:

        @pl.when(plane == at)
        def _():
            for copy in down_copies(p):
                copy.start()

    for copy in far:
        copy.wait()
    gain = gain_ref[...].astype(F32)
    half = total_ref.shape[0] // 2
    local = half // GROUP
    line = local + 8
    dims = (((1,), (1,)), ((), ()))
    gains = None
    for out_ref, k in ((send_ref, 1 - core), (keep_ref, core)):
        for h in range(0, GROUP, 2):
            own_rows = pl.ds(pl.multiple_of(k * half + h * local, 128), 2 * local)
            total = total_ref[own_rows] + jnp.dot(far_ref[own_rows], weight[...], preferred_element_type=F32)
            stream = total.astype(BF16).astype(F32)
            row_sum = jnp.sum(stream, axis=1, keepdims=True)
            squares = jnp.sum(stream * stream, axis=1, keepdims=True)
            lane = lax.broadcasted_iota(jnp.int32, (2 * local, 128), 1)
            both = jnp.where(lane == 0, row_sum, jnp.where(lane == 1, squares, 0.0)).T
            if gains is None:
                for at, p in ends:

                    @pl.when(plane == at)
                    def _():
                        for copy in down_copies(p):
                            copy.wait()

                gains = jnp.broadcast_to(gain_ref[...], (16, gain_ref.shape[1]))
                gains = lax.dot_general(gains, down[...], dims, preferred_element_type=F32)[:8]
            scaled = (stream * gain).astype(BF16)
            value = lax.dot_general(scaled, down[...], dims, preferred_element_type=F32)
            for g in range(2):
                at = (h + g) * line
                out_ref[at : at + local] = value[g * local : (g + 1) * local]
                out_ref[at + local : at + line] = gains
                out_ref[at + local + 1 : at + local + 3, :local] = both[:2, g * local : (g + 1) * local]


def finish(rows, planes, total, far, gain, near, flow):
    count = total.shape[1]
    tokens = total.shape[0]
    span = flow[0].shape[0]
    out = (span - rows) * GROUP * planes
    inside = pl.BlockSpec(memory_space=pltpu.VMEM)
    return pl.pallas_call(
        functools.partial(finish_kernel, rows, planes),
        in_specs=[inside] * 4 + [pl.BlockSpec(memory_space=pl.ANY)] * len(flow),
        out_specs=[inside, inside],
        out_shape=[jax.ShapeDtypeStruct((tokens // 2 + 8 * GROUP, out), F32)] * 2,
        scratch_shapes=[
            pltpu.VMEM((GROUP * rows, count), BF16),
            pltpu.VMEM((out, count), BF16),
            pltpu.SemaphoreType.DMA((GROUP,)),
            pltpu.SemaphoreType.DMA((GROUP,)),
            pltpu.SemaphoreType.DMA,
        ],
        compiler_params=pltpu.CompilerParams(vmem_limit_bytes=20 << 20),
        cost_estimate=pl.CostEstimate(
            flops=2 * tokens * count * (GROUP * rows + out), bytes_accessed=16 << 20, transcendentals=0
        ),
    )(total, far, gain, near, *flow)


def split(value):
    high = value.astype(BF16)
    return high, (value - high.astype(F32)).astype(BF16)


def times(value, weight, turned=False):
    count = value.shape[0]
    dims = (((1,), (1 if turned else 0,)), ((), ()))
    both = lax.dot_general(jnp.concatenate(split(value), axis=0), weight, dims, preferred_element_type=F32)
    return both[:count] + both[count:]


def outer(left, right):
    (left, left_low), (right, right_low) = split(left), split(right)
    left = jnp.concatenate([left, left, left_low], axis=0)
    right = jnp.concatenate([right, right_low, right], axis=0)
    return lax.dot_general(left, right, (((0,), (0,)), ((), ())), preferred_element_type=F32)


def gelu_and_slope(v):
    scale = 0.7978845608028654
    t = jnp.tanh(scale * (v + 0.044715 * (v * v * v)))
    slope = 0.5 * (1.0 + t) + 0.5 * v * (1.0 - t * t) * (scale * (1.0 + 3.0 * 0.044715 * (v * v)))
    return 0.5 * v * (1.0 + t), slope


def side_kernel(width, all_tokens, *refs):
    *part_refs, f_ref, g_ref, target_ref, out_ref, keep_ref, send_ref = refs
    local, features = out_ref.shape
    half = features // 2
    total = part_refs[0][...]
    for ref in part_refs[1:]:
        total = total + ref[...]
    tail = total[local:]
    stats = jnp.concatenate([tail[:, :local]] * (local // 8), axis=0).T
    mean = stats[:, 1:2] / width
    spread = stats[:, 2:3] / width - mean * mean
    side_in = (total[:local] - mean * tail[:1]) / jnp.sqrt(spread + 1e-06)
    first, second = side_in[:, :half], side_in[:, half:]
    f_w, g_w = f_ref[...], g_ref[...]
    f_value, f_slope = gelu_and_slope(times(second, f_w))
    upper = first + f_value
    g_value, g_slope = gelu_and_slope(times(upper, g_w))
    lower = second + g_value
    out_ref[:, :half] = upper
    out_ref[:, half:] = lower
    g_back = (lower - target_ref[:, half:]) / all_tokens * g_slope
    upper_back = (upper - target_ref[:, :half]) / all_tokens + times(g_back, g_w, turned=True)
    g_grad = outer(upper, g_back)
    f_grad = outer(second, upper_back * f_slope)
    core = lax.axis_index("narrow")

    @pl.when(core == 0)
    def _():
        keep_ref[...] = f_grad
        send_ref[...] = g_grad

    @pl.when(core != 0)
    def _():
        keep_ref[...] = g_grad
        send_ref[...] = f_grad


def side_block(width, all_tokens, parts, f_weight, g_weight, targets):
    inside = pl.BlockSpec(memory_space=pltpu.VMEM)
    grad = jax.ShapeDtypeStruct(f_weight.shape, F32)
    work = targets.shape[0] * f_weight.size
    return pl.pallas_call(
        functools.partial(side_kernel, width, all_tokens),
        in_specs=[inside] * (len(parts) + 3),
        out_specs=[inside] * 3,
        out_shape=[jax.ShapeDtypeStruct(targets.shape, F32), grad, grad],
        compiler_params=pltpu.CompilerParams(vmem_limit_bytes=24 << 20),
        cost_estimate=pl.CostEstimate(flops=24 * work, bytes_accessed=5 << 20, transcendentals=2 * targets.size),
    )(*parts, f_weight, g_weight, targets)


def per_device(group, wides, narrows, context, out_weight, residual, ln_gain, side_down, f_weight, g_weight, targets):
    planes = wides // group
    wide, core = lax.axis_index("wide"), lax.axis_index("narrow")
    plane, member = wide // group, wide % group
    short = group == GROUP and planes == 4 and narrows == 2
    features = out_weight.shape[1] // group
    rows = out_weight.shape[0]
    tokens = context.shape[0]
    local = tokens // narrows
    members = range(group)
    cores = range(narrows)

    def to_member(value, s):
        pairs = [(i, i - i % group + (i % group ^ s)) for i in range(wides)]
        return lax.ppermute(value, "wide", pairs) if s else value

    def to_core(value, t):
        return lax.ppermute(value, "narrow", [(i, i ^ t) for i in range(narrows)]) if t else value

    def block(value, index, size, axis):
        return lax.dynamic_slice_in_dim(value, index * size, size, axis)

    def sum_cores(pick):
        total = pick(core)
        for t in range(1, narrows):
            total = total + to_core(pick(core ^ t), t)
        return total

    def sum_members(pick):
        total = pick(0)
        for s in range(1, group):
            total = total + to_member(pick(s), s)
        return total

    own = [block(out_weight, member ^ s, features, 1) for s in members]
    down_own = [block(side_down.T, member ^ s, features, 1) for s in members]
    stay_own = [block(residual, member ^ s, features, 1) for s in members]
    gain = block(ln_gain, member, features, 0)[None, :]
    columns = down_own[0].shape[0]
    side_rows = group * local

    def in_plane(downs):
        value = jnp.zeros((group * columns, features), BF16)
        for s in members:
            value = lax.dynamic_update_slice_in_dim(value, downs[s], (member ^ s) * columns, 0)
        return value

    if short:
        own = [jnp.concatenate(pair, axis=0) for pair in zip(own, down_own)]
        boxes = [jnp.concatenate([context, value], axis=1) for value in stay_own[1:]]

        def line(value, pairs):
            pairs = [(i * group + m, j * group + m) for i, j in pairs for m in members]
            return lax.ppermute(value, "wide", pairs)

        outward, inward = [(1, 0), (2, 3)], [(1, 2), (2, 1)]

        def step_one(value):
            return line(value, outward + [(0, 1), (3, 2)]), line(value, inward)

        def step_two(first, second):
            return line(first, inward), line(second, outward)

        own_one = step_one(own[0])
        own_two = step_two(*own_one)
        rest = jnp.concatenate([to_member(own[s], s) for s in range(1, group)], axis=0)

        rest, boxes, own_two = lax.optimization_barrier((rest, boxes, own_two))
        rest_one = step_one(rest)
        own_last = line(own_two[0], outward)
        arrived = [to_member(boxes[0], 1), to_member(boxes[1], 2)]

        arrived, boxes, rest_one, own_last = lax.optimization_barrier((arrived, boxes, rest_one, own_last))
        rest_two = step_two(*rest_one)
        arrived.append(to_member(boxes[2], 3))
        heads = context.shape[1]
        part = jnp.concatenate([context] + [v[:, :heads] for v in arrived[:2]] + [jnp.zeros_like(context)], axis=0)
        stay = stay_own[:1] + [v[:, heads:] for v in arrived[:2]]

        box, part, stay, rest_two = lax.optimization_barrier((arrived[2], part, stay, rest_two))
        rest_last = line(rest_two[0], outward)
        part = lax.dynamic_update_slice_in_dim(part, box[:, :heads], 3 * tokens, 0)
        stay.append(box[:, heads:])
        mine, other = [v.reshape(group, tokens, -1) for v in (part, to_core(part, 1))]
        flow = [own[0], rest]
        for pair in zip(own_one + own_two, rest_one + rest_two):
            flow += pair
        total, near_down = attend(rows, planes, mine, other, stay, flow)
        last = jnp.where(plane == 0, planes - 1, 0)
        width = group * rows
        last_part = jnp.where(last * width // heads == core, mine, other)
        last_part = lax.dynamic_slice_in_dim(last_part, last * width % heads, width, 2)
        last_part = last_part.reshape(group, narrows, local, width).swapaxes(0, 1).reshape(-1, width)
        flow = [own_last, rest_last]
        keep, send = finish(rows, planes, total, last_part, gain, near_down, flow)
        summed = keep + to_core(send, 1)
        span = local + 8
        pieces = [summed[:span]]
        pieces += [to_member(summed[s * span : (s + 1) * span], s) for s in range(1, group)]
        width = out_weight.shape[1] * narrows
        all_tokens = local * wides * narrows
        side_out, keep, send = side_block(width, all_tokens, pieces, f_weight, g_weight, targets)
        grads = keep + to_core(send, 1)
    else:
        pieces = [to_member(own[s], s) for s in members]
        down_plane = in_plane([to_member(down_own[s], s) for s in members])
        arrived = [to_member(context, s) for s in members]
        stay = [to_member(stay_own[s], s) for s in members]
        parts = [to_core(jnp.concatenate(arrived, axis=0), t) for t in cores]
        lines = [[p * group + m for p in range(planes)] for m in range(group)]
        chunk = jnp.zeros((group * rows, features), BF16)
        for s in members:
            chunk = lax.dynamic_update_slice_in_dim(chunk, pieces[s], (member ^ s) * rows, 0)
        weight = lax.all_gather(chunk, "wide", axis_index_groups=lines, tiled=True)
        all_down = lax.all_gather(down_plane, "wide", axis_index_groups=lines, tiled=True)

        def by_core(value):
            value = value.reshape(group, narrows, local, -1)
            return value.swapaxes(0, 1).reshape(group * tokens, -1)

        heads = context.shape[1]
        attn_sum = jnp.zeros((), F32)
        for t in cores:
            share = block(weight, core ^ t, heads, 0)
            attn_sum = attn_sum + jnp.dot(parts[t], share, preferred_element_type=F32)
        stream = (jnp.concatenate(stay, axis=0).astype(F32) + attn_sum).astype(BF16)
        stream = by_core(stream).astype(F32)
        scaled = (stream * gain.astype(F32)).astype(BF16).reshape(narrows, side_rows, features)
        gains = jnp.broadcast_to(gain[None], (narrows, 8, features))
        scaled = jnp.concatenate([scaled, gains], axis=1)
        stats = jnp.stack([jnp.sum(stream, axis=1), jnp.sum(stream * stream, axis=1)])
        stats_own = stats.reshape(2, narrows, group, local)

        def share_of_core(k):
            lhs = lax.dynamic_index_in_dim(scaled, k, 0, keepdims=False)
            return lax.dot_general(lhs, all_down, (((1,), (1,)), ((), ())), preferred_element_type=F32)

        summed = sum_cores(share_of_core)
        tail = summed[side_rows:]
        projected = sum_members(
            lambda s: jnp.concatenate([summed[s * local : (s + 1) * local], tail], axis=0)
        )
        summed_stats = sum_cores(lambda k: lax.dynamic_index_in_dim(stats_own, k, 1, keepdims=False))
        stats = sum_members(lambda s: summed_stats[:, s])
        projected, gain_map = projected[:local], projected[local]

        width = out_weight.shape[1] * narrows
        mean = stats[0] / width
        spread = stats[1] / width - mean * mean
        side_in = (projected - mean[:, None] * gain_map[None, :]) / jnp.sqrt(spread + 1e-06)[:, None]
        half = side_in.shape[1] // 2
        f_w, g_w = f_weight.astype(F32), g_weight.astype(F32)
        first, second = side_in[:, :half], side_in[:, half:]
        f_value, f_pull = jax.vjp(coupling, second, f_w)
        upper = first + f_value
        g_value, g_pull = jax.vjp(coupling, upper, g_w)
        lower = second + g_value
        side_out = jnp.concatenate([upper, lower], axis=1)
        misfit = (side_out - targets) / (local * wides * narrows)
        upper_back, g_local = g_pull(misfit[:, half:])
        f_local = f_pull(misfit[:, :half] + upper_back)[1]
        f_total, g_total = lax.psum((f_local, g_local), ("wide", "narrow"))
        return side_out, f_total, g_total

    half = grads.shape[1]
    share = grads.shape[0] // group
    part = grads
    grads = sum_members(lambda s: block(part, member ^ s, share, 0))
    share = share // planes

    def shift(value, k):
        return lax.ppermute(value, "wide", [(i, (i + k * group) % wides) for i in range(wides)])

    part = grads
    grads = block(part, plane, share, 0)
    for k in range(1, planes):
        grads = grads + shift(block(part, (plane + k) % planes, share, 0), k)
    whole = jnp.zeros((planes * share, half), F32)
    for k in range(planes):
        piece = shift(grads, k) if k else grads
        whole = lax.dynamic_update_slice_in_dim(whole, piece, (plane - k) % planes * share, 0)
    share = share * planes
    part, whole = whole, jnp.zeros((group * share, half), F32)
    for s in members:
        whole = lax.dynamic_update_slice_in_dim(whole, to_member(part, s), (member ^ s) * share, 0)
    other = to_core(whole, 1)
    return side_out, jnp.where(core == 0, whole, other), jnp.where(core == 0, other, whole)


def solution(mesh):
    wides, narrows = mesh.shape["wide"], mesh.shape["narrow"]
    group = GROUP if wides % GROUP == 0 else 1
    in_specs = (
        P("wide", "narrow"),
        P("wide", "narrow"),
        P("wide", "narrow"),
        P("narrow"),
        P("narrow", "wide"),
        P(),
        P(),
        P(("wide", "narrow"), None),
    )
    out_specs = (P(("wide", "narrow"), None), P(), P())
    return jax.shard_map(
        functools.partial(per_device, group, wides, narrows),
        mesh=mesh,
        in_specs=in_specs,
        out_specs=out_specs,
        check_vma=False,
    )
```

```python
import functools

import jax
import jax.numpy as jnp
from jax import lax
from jax.experimental import pallas as pl
from jax.experimental.pallas import tpu as pltpu
from jax.sharding import PartitionSpec as P

HIGH = lax.Precision.HIGH
F32 = jnp.float32
BF16 = jnp.bfloat16
GROUP = 4


def coupling(values, weight):
    return jax.nn.gelu(jnp.dot(values, weight, precision=HIGH))


def place():
    wide, core = lax.axis_index("wide"), lax.axis_index("narrow")
    return wide // GROUP, wide % GROUP, core


ROUTES = ((0, 1, 4, 5), (1, 0, 2, 3), (3, 2, 0, 1), (5, 4, 1, 0))
LAST = 5


def part_of(flow, at, p):
    return flow[2 * ROUTES[at][p] :][:2]


def share_of(pair, s, start, count, span):
    at = start + (s - 1) * span if s else start
    return pair[1 if s else 0].at[pl.ds(at, count)]


def attend_kernel(rows, planes, *refs):
    mine_ref, other_ref, *refs = refs
    stay_refs, (*flow, out_ref, down_ref, weight, sems, down_sems) = refs[:GROUP], refs[GROUP:]
    plane, member, core = place()
    span = flow[0].shape[0]
    columns = span - rows

    for at in range(planes):

        @pl.when((pl.program_id(0) == 0) & (plane == at))
        def _():
            copies = []
            for p in range(planes):
                if ROUTES[at][p] == LAST:
                    weight[p * GROUP * rows : (p + 1) * GROUP * rows] = jnp.zeros((GROUP * rows, weight.shape[1]), BF16)
                    ends = (p * GROUP * columns, (p + 1) * GROUP * columns)
                    down_ref[ends[0] : ends[1]] = jnp.zeros((GROUP * columns, weight.shape[1]), BF16)
                    continue
                for s in range(GROUP):
                    target = pl.multiple_of((p * GROUP + (member ^ s)) * rows, 64)
                    source = share_of(part_of(flow, at, p), s, 0, rows, span)
                    copies.append(pltpu.make_async_copy(source, weight.at[pl.ds(target, rows)], sems.at[p, s]))
                    target = pl.multiple_of((p * GROUP + (member ^ s)) * columns, 16)
                    source = share_of(part_of(flow, at, p), s, rows, columns, span)
                    target = down_ref.at[pl.ds(target, columns)]
                    copies.append(pltpu.make_async_copy(source, target, down_sems.at[p, s]))
            for copy in copies:
                copy.start()
            for copy in copies:
                copy.wait()

    group, local, heads = mine_ref.shape
    for h in range(0, group, 2):
        lhs = mine_ref[h : h + 2].reshape(2 * local, heads)
        rhs = other_ref[h : h + 2].reshape(2 * local, heads)
        at = pl.multiple_of(core * heads, 128)
        total = jnp.dot(lhs, weight[pl.ds(at, heads)], preferred_element_type=F32)
        at = pl.multiple_of((1 - core) * heads, 128)
        total += jnp.dot(rhs, weight[pl.ds(at, heads)], preferred_element_type=F32)
        for g in range(2):
            stay = stay_refs[h + g][...].astype(F32)
            out_ref[(h + g) * local : (h + g + 1) * local] = stay + total[g * local : (g + 1) * local]


def attend(rows, planes, mine, other, stay, flow):
    group, tokens, heads = mine.shape
    count = flow[0].shape[1]
    part = pl.BlockSpec((group, tokens // 2, heads), lambda i: (0, i, 0))
    out = (flow[0].shape[0] - rows) * group * planes
    return pl.pallas_call(
        functools.partial(attend_kernel, rows, planes),
        grid=(2,),
        in_specs=[part, part]
        + [pl.BlockSpec((tokens // 2, count), lambda i: (i, 0))] * group
        + [pl.BlockSpec(memory_space=pl.ANY)] * len(flow),
        out_specs=[
            pl.BlockSpec((group * tokens // 2, count), lambda i: (i, 0)),
            pl.BlockSpec((out, count), lambda i: (0, 0)),
        ],
        out_shape=[
            jax.ShapeDtypeStruct((group * tokens, count), F32),
            jax.ShapeDtypeStruct((out, count), BF16),
        ],
        scratch_shapes=[
            pltpu.VMEM((2 * heads, count), BF16),
            pltpu.SemaphoreType.DMA((planes, group)),
            pltpu.SemaphoreType.DMA((planes, group)),
        ],
        compiler_params=pltpu.CompilerParams(vmem_limit_bytes=28 << 20),
        cost_estimate=pl.CostEstimate(
            flops=4 * group * tokens * heads * count, bytes_accessed=16 << 20, transcendentals=0
        ),
    )(mine, other, *stay, *flow)


def finish_kernel(rows, planes, *refs):
    total_ref, far_ref, gain_ref, near_ref, *flow, keep_ref, send_ref, weight, down, sems, down_sems, near_sem = refs
    plane, member, core = place()
    span = flow[0].shape[0]
    columns = span - rows

    def far_copies():
        out = []
        for s in range(GROUP):
            target = pl.multiple_of((member ^ s) * rows, 64)
            source = share_of(flow, s, 0, rows, span)
            out.append(pltpu.make_async_copy(source, weight.at[pl.ds(target, rows)], sems.at[s]))
        return out

    def down_copies(p):
        out = []
        for s in range(GROUP):
            target = pl.multiple_of((p * GROUP + (member ^ s)) * columns, 16)
            source = share_of(flow, s, rows, columns, span)
            out.append(pltpu.make_async_copy(source, down.at[pl.ds(target, columns)], down_sems.at[s]))
        return out

    near = pltpu.make_async_copy(near_ref, down, near_sem)
    near.start()
    far = far_copies()
    for copy in far:
        copy.start()
    near.wait()
    ends = [(at, ROUTES[at].index(LAST)) for at in range(planes) if LAST in ROUTES[at]]
    for at, p in ends:

        @pl.when(plane == at)
        def _():
            for copy in down_copies(p):
                copy.start()

    for copy in far:
        copy.wait()
    gain = gain_ref[...].astype(F32)
    half = total_ref.shape[0] // 2
    local = half // GROUP
    line = local + 8
    dims = (((1,), (1,)), ((), ()))
    gains = None
    for out_ref, k in ((send_ref, 1 - core), (keep_ref, core)):
        for h in range(0, GROUP, 2):
            own_rows = pl.ds(pl.multiple_of(k * half + h * local, 128), 2 * local)
            total = total_ref[own_rows] + jnp.dot(far_ref[own_rows], weight[...], preferred_element_type=F32)
            stream = total.astype(BF16).astype(F32)
            row_sum = jnp.sum(stream, axis=1, keepdims=True)
            squares = jnp.sum(stream * stream, axis=1, keepdims=True)
            lane = lax.broadcasted_iota(jnp.int32, (2 * local, 128), 1)
            both = jnp.where(lane == 0, row_sum, jnp.where(lane == 1, squares, 0.0)).T
            if gains is None:
                for at, p in ends:

                    @pl.when(plane == at)
                    def _():
                        for copy in down_copies(p):
                            copy.wait()

                gains = jnp.broadcast_to(gain_ref[...], (16, gain_ref.shape[1]))
                gains = lax.dot_general(gains, down[...], dims, preferred_element_type=F32)[:8]
            scaled = (stream * gain).astype(BF16)
            value = lax.dot_general(scaled, down[...], dims, preferred_element_type=F32)
            for g in range(2):
                at = (h + g) * line
                out_ref[at : at + local] = value[g * local : (g + 1) * local]
                out_ref[at + local : at + line] = gains
                out_ref[at + local + 1 : at + local + 3, :local] = both[:2, g * local : (g + 1) * local]


def finish(rows, planes, total, far, gain, near, flow):
    count = total.shape[1]
    tokens = total.shape[0]
    span = flow[0].shape[0]
    out = (span - rows) * GROUP * planes
    inside = pl.BlockSpec(memory_space=pltpu.VMEM)
    return pl.pallas_call(
        functools.partial(finish_kernel, rows, planes),
        in_specs=[inside] * 4 + [pl.BlockSpec(memory_space=pl.ANY)] * len(flow),
        out_specs=[inside, inside],
        out_shape=[jax.ShapeDtypeStruct((tokens // 2 + 8 * GROUP, out), F32)] * 2,
        scratch_shapes=[
            pltpu.VMEM((GROUP * rows, count), BF16),
            pltpu.VMEM((out, count), BF16),
            pltpu.SemaphoreType.DMA((GROUP,)),
            pltpu.SemaphoreType.DMA((GROUP,)),
            pltpu.SemaphoreType.DMA,
        ],
        compiler_params=pltpu.CompilerParams(vmem_limit_bytes=20 << 20),
        cost_estimate=pl.CostEstimate(
            flops=2 * tokens * count * (GROUP * rows + out), bytes_accessed=16 << 20, transcendentals=0
        ),
    )(total, far, gain, near, *flow)


def split(value):
    high = value.astype(BF16)
    return high, (value - high.astype(F32)).astype(BF16)


def times(value, weight, turned=False):
    count = value.shape[0]
    dims = (((1,), (1 if turned else 0,)), ((), ()))
    both = lax.dot_general(jnp.concatenate(split(value), axis=0), weight, dims, preferred_element_type=F32)
    return both[:count] + both[count:]


def outer(left, right):
    (left, left_low), (right, right_low) = split(left), split(right)
    left = jnp.concatenate([left, left, left_low], axis=0)
    right = jnp.concatenate([right, right_low, right], axis=0)
    return lax.dot_general(left, right, (((0,), (0,)), ((), ())), preferred_element_type=F32)


def gelu_and_slope(v):
    scale = 0.7978845608028654
    t = jnp.tanh(scale * (v + 0.044715 * (v * v * v)))
    slope = 0.5 * (1.0 + t) + 0.5 * v * (1.0 - t * t) * (scale * (1.0 + 3.0 * 0.044715 * (v * v)))
    return 0.5 * v * (1.0 + t), slope


def side_kernel(width, all_tokens, *refs):
    *part_refs, f_ref, g_ref, target_ref, out_ref, keep_ref, send_ref = refs
    local, features = out_ref.shape
    half = features // 2
    total = part_refs[0][...]
    for ref in part_refs[1:]:
        total = total + ref[...]
    tail = total[local:]
    stats = jnp.concatenate([tail[:, :local]] * (local // 8), axis=0).T
    mean = stats[:, 1:2] / width
    spread = stats[:, 2:3] / width - mean * mean
    side_in = (total[:local] - mean * tail[:1]) / jnp.sqrt(spread + 1e-06)
    first, second = side_in[:, :half], side_in[:, half:]
    f_w, g_w = f_ref[...], g_ref[...]
    f_value, f_slope = gelu_and_slope(times(second, f_w))
    upper = first + f_value
    g_value, g_slope = gelu_and_slope(times(upper, g_w))
    lower = second + g_value
    out_ref[:, :half] = upper
    out_ref[:, half:] = lower
    g_back = (lower - target_ref[:, half:]) / all_tokens * g_slope
    upper_back = (upper - target_ref[:, :half]) / all_tokens + times(g_back, g_w, turned=True)
    g_grad = outer(upper, g_back)
    f_grad = outer(second, upper_back * f_slope)
    core = lax.axis_index("narrow")

    @pl.when(core == 0)
    def _():
        keep_ref[...] = f_grad
        send_ref[...] = g_grad

    @pl.when(core != 0)
    def _():
        keep_ref[...] = g_grad
        send_ref[...] = f_grad


def side_block(width, all_tokens, parts, f_weight, g_weight, targets):
    inside = pl.BlockSpec(memory_space=pltpu.VMEM)
    grad = jax.ShapeDtypeStruct(f_weight.shape, F32)
    work = targets.shape[0] * f_weight.size
    return pl.pallas_call(
        functools.partial(side_kernel, width, all_tokens),
        in_specs=[inside] * (len(parts) + 3),
        out_specs=[inside] * 3,
        out_shape=[jax.ShapeDtypeStruct(targets.shape, F32), grad, grad],
        compiler_params=pltpu.CompilerParams(vmem_limit_bytes=24 << 20),
        cost_estimate=pl.CostEstimate(flops=24 * work, bytes_accessed=5 << 20, transcendentals=2 * targets.size),
    )(*parts, f_weight, g_weight, targets)


def per_device(group, wides, narrows, context, out_weight, residual, ln_gain, side_down, f_weight, g_weight, targets):
    planes = wides // group
    wide, core = lax.axis_index("wide"), lax.axis_index("narrow")
    plane, member = wide // group, wide % group
    short = group == GROUP and planes == 4 and narrows == 2
    features = out_weight.shape[1] // group
    rows = out_weight.shape[0]
    tokens = context.shape[0]
    local = tokens // narrows
    members = range(group)
    cores = range(narrows)

    def to_member(value, s):
        pairs = [(i, i - i % group + (i % group ^ s)) for i in range(wides)]
        return lax.ppermute(value, "wide", pairs) if s else value

    def to_core(value, t):
        return lax.ppermute(value, "narrow", [(i, i ^ t) for i in range(narrows)]) if t else value

    def block(value, index, size, axis):
        return lax.dynamic_slice_in_dim(value, index * size, size, axis)

    def sum_cores(pick):
        total = pick(core)
        for t in range(1, narrows):
            total = total + to_core(pick(core ^ t), t)
        return total

    def sum_members(pick):
        total = pick(0)
        for s in range(1, group):
            total = total + to_member(pick(s), s)
        return total

    own = [block(out_weight, member ^ s, features, 1) for s in members]
    down_own = [block(side_down.T, member ^ s, features, 1) for s in members]
    stay_own = [block(residual, member ^ s, features, 1) for s in members]
    gain = block(ln_gain, member, features, 0)[None, :]
    columns = down_own[0].shape[0]
    side_rows = group * local

    def in_plane(downs):
        value = jnp.zeros((group * columns, features), BF16)
        for s in members:
            value = lax.dynamic_update_slice_in_dim(value, downs[s], (member ^ s) * columns, 0)
        return value

    if short:
        own = [jnp.concatenate(pair, axis=0) for pair in zip(own, down_own)]
        boxes = [jnp.concatenate([context, value], axis=1) for value in stay_own[1:]]

        def line(value, pairs):
            pairs = [(i * group + m, j * group + m) for i, j in pairs for m in members]
            return lax.ppermute(value, "wide", pairs)

        outward, inward = [(1, 0), (2, 3)], [(1, 2), (2, 1)]

        def step_one(value):
            return line(value, outward + [(0, 1), (3, 2)]), line(value, inward)

        def step_two(first, second):
            return line(first, inward), line(second, outward)

        own_one = step_one(own[0])
        own_two = step_two(*own_one)
        rest = jnp.concatenate([to_member(own[s], s) for s in range(1, group)], axis=0)

        rest_one = step_one(rest)
        _, boxes, own_two = lax.optimization_barrier((rest, boxes, own_two))
        own_last = line(own_two[0], outward)
        arrived = [to_member(boxes[0], 1), to_member(boxes[1], 2)]

        rest_two = step_two(*rest_one)
        arrived, boxes, _, own_last = lax.optimization_barrier((arrived, boxes, rest_one, own_last))
        arrived.append(to_member(boxes[2], 3))
        heads = context.shape[1]
        part = jnp.concatenate([context] + [v[:, :heads] for v in arrived[:2]] + [jnp.zeros_like(context)], axis=0)
        stay = stay_own[:1] + [v[:, heads:] for v in arrived[:2]]

        box, part, stay, rest_two = lax.optimization_barrier((arrived[2], part, stay, rest_two))
        rest_last = line(rest_two[0], outward)
        part = lax.dynamic_update_slice_in_dim(part, box[:, :heads], 3 * tokens, 0)
        stay.append(box[:, heads:])
        mine, other = [v.reshape(group, tokens, -1) for v in (part, to_core(part, 1))]
        flow = [own[0], rest]
        for pair in zip(own_one + own_two, rest_one + rest_two):
            flow += pair
        total, near_down = attend(rows, planes, mine, other, stay, flow)
        last = jnp.where(plane == 0, planes - 1, 0)
        width = group * rows
        last_part = jnp.where(last * width // heads == core, mine, other)
        last_part = lax.dynamic_slice_in_dim(last_part, last * width % heads, width, 2)
        last_part = last_part.reshape(group, narrows, local, width).swapaxes(0, 1).reshape(-1, width)
        flow = [own_last, rest_last]
        keep, send = finish(rows, planes, total, last_part, gain, near_down, flow)
        summed = keep + to_core(send, 1)
        span = local + 8
        pieces = [summed[:span]]
        pieces += [to_member(summed[s * span : (s + 1) * span], s) for s in range(1, group)]
        width = out_weight.shape[1] * narrows
        all_tokens = local * wides * narrows
        side_out, keep, send = side_block(width, all_tokens, pieces, f_weight, g_weight, targets)
        grads = keep + to_core(send, 1)
    else:
        pieces = [to_member(own[s], s) for s in members]
        down_plane = in_plane([to_member(down_own[s], s) for s in members])
        arrived = [to_member(context, s) for s in members]
        stay = [to_member(stay_own[s], s) for s in members]
        parts = [to_core(jnp.concatenate(arrived, axis=0), t) for t in cores]
        lines = [[p * group + m for p in range(planes)] for m in range(group)]
        chunk = jnp.zeros((group * rows, features), BF16)
        for s in members:
            chunk = lax.dynamic_update_slice_in_dim(chunk, pieces[s], (member ^ s) * rows, 0)
        weight = lax.all_gather(chunk, "wide", axis_index_groups=lines, tiled=True)
        all_down = lax.all_gather(down_plane, "wide", axis_index_groups=lines, tiled=True)

        def by_core(value):
            value = value.reshape(group, narrows, local, -1)
            return value.swapaxes(0, 1).reshape(group * tokens, -1)

        heads = context.shape[1]
        attn_sum = jnp.zeros((), F32)
        for t in cores:
            share = block(weight, core ^ t, heads, 0)
            attn_sum = attn_sum + jnp.dot(parts[t], share, preferred_element_type=F32)
        stream = (jnp.concatenate(stay, axis=0).astype(F32) + attn_sum).astype(BF16)
        stream = by_core(stream).astype(F32)
        scaled = (stream * gain.astype(F32)).astype(BF16).reshape(narrows, side_rows, features)
        gains = jnp.broadcast_to(gain[None], (narrows, 8, features))
        scaled = jnp.concatenate([scaled, gains], axis=1)
        stats = jnp.stack([jnp.sum(stream, axis=1), jnp.sum(stream * stream, axis=1)])
        stats_own = stats.reshape(2, narrows, group, local)

        def share_of_core(k):
            lhs = lax.dynamic_index_in_dim(scaled, k, 0, keepdims=False)
            return lax.dot_general(lhs, all_down, (((1,), (1,)), ((), ())), preferred_element_type=F32)

        summed = sum_cores(share_of_core)
        tail = summed[side_rows:]
        projected = sum_members(
            lambda s: jnp.concatenate([summed[s * local : (s + 1) * local], tail], axis=0)
        )
        summed_stats = sum_cores(lambda k: lax.dynamic_index_in_dim(stats_own, k, 1, keepdims=False))
        stats = sum_members(lambda s: summed_stats[:, s])
        projected, gain_map = projected[:local], projected[local]

        width = out_weight.shape[1] * narrows
        mean = stats[0] / width
        spread = stats[1] / width - mean * mean
        side_in = (projected - mean[:, None] * gain_map[None, :]) / jnp.sqrt(spread + 1e-06)[:, None]
        half = side_in.shape[1] // 2
        f_w, g_w = f_weight.astype(F32), g_weight.astype(F32)
        first, second = side_in[:, :half], side_in[:, half:]
        f_value, f_pull = jax.vjp(coupling, second, f_w)
        upper = first + f_value
        g_value, g_pull = jax.vjp(coupling, upper, g_w)
        lower = second + g_value
        side_out = jnp.concatenate([upper, lower], axis=1)
        misfit = (side_out - targets) / (local * wides * narrows)
        upper_back, g_local = g_pull(misfit[:, half:])
        f_local = f_pull(misfit[:, :half] + upper_back)[1]
        f_total, g_total = lax.psum((f_local, g_local), ("wide", "narrow"))
        return side_out, f_total, g_total

    half = grads.shape[1]
    share = grads.shape[0] // group
    part = grads
    grads = sum_members(lambda s: block(part, member ^ s, share, 0))
    share = share // planes

    def shift(value, k):
        return lax.ppermute(value, "wide", [(i, (i + k * group) % wides) for i in range(wides)])

    part = grads
    grads = block(part, plane, share, 0)
    for k in range(1, planes):
        grads = grads + shift(block(part, (plane + k) % planes, share, 0), k)
    whole = jnp.zeros((planes * share, half), F32)
    for k in range(planes):
        piece = shift(grads, k) if k else grads
        whole = lax.dynamic_update_slice_in_dim(whole, piece, (plane - k) % planes * share, 0)
    share = share * planes
    part, whole = whole, jnp.zeros((group * share, half), F32)
    for s in members:
        whole = lax.dynamic_update_slice_in_dim(whole, to_member(part, s), (member ^ s) * share, 0)
    other = to_core(whole, 1)
    return side_out, jnp.where(core == 0, whole, other), jnp.where(core == 0, other, whole)


def solution(mesh):
    wides, narrows = mesh.shape["wide"], mesh.shape["narrow"]
    group = GROUP if wides % GROUP == 0 else 1
    in_specs = (
        P("wide", "narrow"),
        P("wide", "narrow"),
        P("wide", "narrow"),
        P("narrow"),
        P("narrow", "wide"),
        P(),
        P(),
        P(("wide", "narrow"), None),
    )
    out_specs = (P(("wide", "narrow"), None), P(), P())
    return jax.shard_map(
        functools.partial(per_device, group, wides, narrows),
        mesh=mesh,
        in_specs=in_specs,
        out_specs=out_specs,
        check_vma=False,
    )
```

```python
import functools

import jax
import jax.numpy as jnp
from jax import lax
from jax.experimental import pallas as pl
from jax.experimental.pallas import tpu as pltpu
from jax.sharding import PartitionSpec as P

HIGH = lax.Precision.HIGH
F32 = jnp.float32
BF16 = jnp.bfloat16
GROUP = 4


def coupling(values, weight):
    return jax.nn.gelu(jnp.dot(values, weight, precision=HIGH))


def place():
    wide, core = lax.axis_index("wide"), lax.axis_index("narrow")
    return wide // GROUP, wide % GROUP, core


ROUTES = ((0, 1, 4, 5), (1, 0, 2, 3), (3, 2, 0, 1), (5, 4, 1, 0))
LAST = 5


def part_of(flow, at, p):
    return flow[2 * ROUTES[at][p] :][:2]


def share_of(pair, s, start, count, span):
    at = start + (s - 1) * span if s else start
    return pair[1 if s else 0].at[pl.ds(at, count)]


def attend_kernel(rows, planes, *refs):
    mine_ref, other_ref, *refs = refs
    stay_refs, (*flow, out_ref, down_ref, weight, sems, down_sems) = refs[:GROUP], refs[GROUP:]
    plane, member, core = place()
    span = flow[0].shape[0]
    columns = span - rows

    for at in range(planes):

        @pl.when((pl.program_id(0) == 0) & (plane == at))
        def _():
            copies = []
            for p in range(planes):
                if ROUTES[at][p] == LAST:
                    weight[p * GROUP * rows : (p + 1) * GROUP * rows] = jnp.zeros((GROUP * rows, weight.shape[1]), BF16)
                    ends = (p * GROUP * columns, (p + 1) * GROUP * columns)
                    down_ref[ends[0] : ends[1]] = jnp.zeros((GROUP * columns, weight.shape[1]), BF16)
                    continue
                for s in range(GROUP):
                    target = pl.multiple_of((p * GROUP + (member ^ s)) * rows, 64)
                    source = share_of(part_of(flow, at, p), s, 0, rows, span)
                    copies.append(pltpu.make_async_copy(source, weight.at[pl.ds(target, rows)], sems.at[p, s]))
                    target = pl.multiple_of((p * GROUP + (member ^ s)) * columns, 16)
                    source = share_of(part_of(flow, at, p), s, rows, columns, span)
                    target = down_ref.at[pl.ds(target, columns)]
                    copies.append(pltpu.make_async_copy(source, target, down_sems.at[p, s]))
            for copy in copies:
                copy.start()
            for copy in copies:
                copy.wait()

    group, local, heads = mine_ref.shape
    for h in range(0, group, 2):
        lhs = mine_ref[h : h + 2].reshape(2 * local, heads)
        rhs = other_ref[h : h + 2].reshape(2 * local, heads)
        at = pl.multiple_of(core * heads, 128)
        total = jnp.dot(lhs, weight[pl.ds(at, heads)], preferred_element_type=F32)
        at = pl.multiple_of((1 - core) * heads, 128)
        total += jnp.dot(rhs, weight[pl.ds(at, heads)], preferred_element_type=F32)
        for g in range(2):
            stay = stay_refs[h + g][...].astype(F32)
            out_ref[(h + g) * local : (h + g + 1) * local] = stay + total[g * local : (g + 1) * local]


def attend(rows, planes, mine, other, stay, flow):
    group, tokens, heads = mine.shape
    count = flow[0].shape[1]
    part = pl.BlockSpec((group, tokens // 2, heads), lambda i: (0, i, 0))
    out = (flow[0].shape[0] - rows) * group * planes
    return pl.pallas_call(
        functools.partial(attend_kernel, rows, planes),
        grid=(2,),
        in_specs=[part, part]
        + [pl.BlockSpec((tokens // 2, count), lambda i: (i, 0))] * group
        + [pl.BlockSpec(memory_space=pl.ANY)] * len(flow),
        out_specs=[
            pl.BlockSpec((group * tokens // 2, count), lambda i: (i, 0)),
            pl.BlockSpec((out, count), lambda i: (0, 0)),
        ],
        out_shape=[
            jax.ShapeDtypeStruct((group * tokens, count), F32),
            jax.ShapeDtypeStruct((out, count), BF16),
        ],
        scratch_shapes=[
            pltpu.VMEM((2 * heads, count), BF16),
            pltpu.SemaphoreType.DMA((planes, group)),
            pltpu.SemaphoreType.DMA((planes, group)),
        ],
        compiler_params=pltpu.CompilerParams(vmem_limit_bytes=26 << 20),
        cost_estimate=pl.CostEstimate(
            flops=4 * group * tokens * heads * count, bytes_accessed=16 << 20, transcendentals=0
        ),
    )(mine, other, *stay, *flow)


def finish_kernel(rows, planes, *refs):
    total_ref, far_ref, gain_ref, near_ref, *flow, keep_ref, send_ref, weight, down, sems, down_sems, near_sem = refs
    plane, member, core = place()
    span = flow[0].shape[0]
    columns = span - rows

    def far_copies():
        out = []
        for s in range(GROUP):
            target = pl.multiple_of((member ^ s) * rows, 64)
            source = share_of(flow, s, 0, rows, span)
            out.append(pltpu.make_async_copy(source, weight.at[pl.ds(target, rows)], sems.at[s]))
        return out

    def down_copies(p):
        out = []
        for s in range(GROUP):
            target = pl.multiple_of((p * GROUP + (member ^ s)) * columns, 16)
            source = share_of(flow, s, rows, columns, span)
            out.append(pltpu.make_async_copy(source, down.at[pl.ds(target, columns)], down_sems.at[s]))
        return out

    near = pltpu.make_async_copy(near_ref, down, near_sem)
    near.start()
    far = far_copies()
    for copy in far:
        copy.start()
    near.wait()
    ends = [(at, ROUTES[at].index(LAST)) for at in range(planes) if LAST in ROUTES[at]]
    for at, p in ends:

        @pl.when(plane == at)
        def _():
            for copy in down_copies(p):
                copy.start()

    for copy in far:
        copy.wait()
    gain = gain_ref[...].astype(F32)
    half = total_ref.shape[0] // 2
    local = half // GROUP
    line = local + 8
    dims = (((1,), (1,)), ((), ()))
    gains = None
    for out_ref, k in ((send_ref, 1 - core), (keep_ref, core)):
        for h in range(0, GROUP, 2):
            own_rows = pl.ds(pl.multiple_of(k * half + h * local, 128), 2 * local)
            total = total_ref[own_rows] + jnp.dot(far_ref[own_rows], weight[...], preferred_element_type=F32)
            stream = total.astype(BF16).astype(F32)
            row_sum = jnp.sum(stream, axis=1, keepdims=True)
            squares = jnp.sum(stream * stream, axis=1, keepdims=True)
            lane = lax.broadcasted_iota(jnp.int32, (2 * local, 128), 1)
            both = jnp.where(lane == 0, row_sum, jnp.where(lane == 1, squares, 0.0)).T
            if gains is None:
                for at, p in ends:

                    @pl.when(plane == at)
                    def _():
                        for copy in down_copies(p):
                            copy.wait()

                gains = jnp.broadcast_to(gain_ref[...], (16, gain_ref.shape[1]))
                gains = lax.dot_general(gains, down[...], dims, preferred_element_type=F32)[:8]
            scaled = (stream * gain).astype(BF16)
            value = lax.dot_general(scaled, down[...], dims, preferred_element_type=F32)
            for g in range(2):
                at = (h + g) * line
                out_ref[at : at + local] = value[g * local : (g + 1) * local]
                out_ref[at + local : at + line] = gains
                out_ref[at + local + 1 : at + local + 3, :local] = both[:2, g * local : (g + 1) * local]


def finish(rows, planes, total, far, gain, near, flow):
    count = total.shape[1]
    tokens = total.shape[0]
    span = flow[0].shape[0]
    out = (span - rows) * GROUP * planes
    inside = pl.BlockSpec(memory_space=pltpu.VMEM)
    return pl.pallas_call(
        functools.partial(finish_kernel, rows, planes),
        in_specs=[inside] * 4 + [pl.BlockSpec(memory_space=pl.ANY)] * len(flow),
        out_specs=[inside, inside],
        out_shape=[jax.ShapeDtypeStruct((tokens // 2 + 8 * GROUP, out), F32)] * 2,
        scratch_shapes=[
            pltpu.VMEM((GROUP * rows, count), BF16),
            pltpu.VMEM((out, count), BF16),
            pltpu.SemaphoreType.DMA((GROUP,)),
            pltpu.SemaphoreType.DMA((GROUP,)),
            pltpu.SemaphoreType.DMA,
        ],
        compiler_params=pltpu.CompilerParams(vmem_limit_bytes=20 << 20),
        cost_estimate=pl.CostEstimate(
            flops=2 * tokens * count * (GROUP * rows + out), bytes_accessed=16 << 20, transcendentals=0
        ),
    )(total, far, gain, near, *flow)


def split(value):
    high = value.astype(BF16)
    return high, (value - high.astype(F32)).astype(BF16)


def times(value, weight, turned=False):
    count = value.shape[0]
    dims = (((1,), (1 if turned else 0,)), ((), ()))
    both = lax.dot_general(jnp.concatenate(split(value), axis=0), weight, dims, preferred_element_type=F32)
    return both[:count] + both[count:]


def outer(left, right):
    (left, left_low), (right, right_low) = split(left), split(right)
    left = jnp.concatenate([left, left, left_low], axis=0)
    right = jnp.concatenate([right, right_low, right], axis=0)
    return lax.dot_general(left, right, (((0,), (0,)), ((), ())), preferred_element_type=F32)


def gelu_and_slope(v):
    scale = 0.7978845608028654
    t = jnp.tanh(scale * (v + 0.044715 * (v * v * v)))
    slope = 0.5 * (1.0 + t) + 0.5 * v * (1.0 - t * t) * (scale * (1.0 + 3.0 * 0.044715 * (v * v)))
    return 0.5 * v * (1.0 + t), slope


def side_kernel(width, all_tokens, *refs):
    *part_refs, f_ref, g_ref, target_ref, out_ref, keep_ref, send_ref = refs
    local, features = out_ref.shape
    half = features // 2
    total = part_refs[0][...]
    for ref in part_refs[1:]:
        total = total + ref[...]
    tail = total[local:]
    stats = jnp.concatenate([tail[:, :local]] * (local // 8), axis=0).T
    mean = stats[:, 1:2] / width
    spread = stats[:, 2:3] / width - mean * mean
    side_in = (total[:local] - mean * tail[:1]) / jnp.sqrt(spread + 1e-06)
    first, second = side_in[:, :half], side_in[:, half:]
    f_w, g_w = f_ref[...], g_ref[...]
    f_value, f_slope = gelu_and_slope(times(second, f_w))
    upper = first + f_value
    g_value, g_slope = gelu_and_slope(times(upper, g_w))
    lower = second + g_value
    out_ref[:, :half] = upper
    out_ref[:, half:] = lower
    g_back = (lower - target_ref[:, half:]) / all_tokens * g_slope
    upper_back = (upper - target_ref[:, :half]) / all_tokens + times(g_back, g_w, turned=True)
    g_grad = outer(upper, g_back)
    f_grad = outer(second, upper_back * f_slope)
    core = lax.axis_index("narrow")

    @pl.when(core == 0)
    def _():
        keep_ref[...] = f_grad
        send_ref[...] = g_grad

    @pl.when(core != 0)
    def _():
        keep_ref[...] = g_grad
        send_ref[...] = f_grad


def side_block(width, all_tokens, parts, f_weight, g_weight, targets):
    inside = pl.BlockSpec(memory_space=pltpu.VMEM)
    grad = jax.ShapeDtypeStruct(f_weight.shape, F32)
    work = targets.shape[0] * f_weight.size
    return pl.pallas_call(
        functools.partial(side_kernel, width, all_tokens),
        in_specs=[inside] * (len(parts) + 3),
        out_specs=[inside] * 3,
        out_shape=[jax.ShapeDtypeStruct(targets.shape, F32), grad, grad],
        compiler_params=pltpu.CompilerParams(vmem_limit_bytes=24 << 20),
        cost_estimate=pl.CostEstimate(flops=24 * work, bytes_accessed=5 << 20, transcendentals=2 * targets.size),
    )(*parts, f_weight, g_weight, targets)


def per_device(group, wides, narrows, context, out_weight, residual, ln_gain, side_down, f_weight, g_weight, targets):
    planes = wides // group
    wide, core = lax.axis_index("wide"), lax.axis_index("narrow")
    plane, member = wide // group, wide % group
    short = group == GROUP and planes == 4 and narrows == 2
    features = out_weight.shape[1] // group
    rows = out_weight.shape[0]
    tokens = context.shape[0]
    local = tokens // narrows
    members = range(group)
    cores = range(narrows)

    def to_member(value, s):
        pairs = [(i, i - i % group + (i % group ^ s)) for i in range(wides)]
        return lax.ppermute(value, "wide", pairs) if s else value

    def to_core(value, t):
        return lax.ppermute(value, "narrow", [(i, i ^ t) for i in range(narrows)]) if t else value

    def block(value, index, size, axis):
        return lax.dynamic_slice_in_dim(value, index * size, size, axis)

    def sum_cores(pick):
        total = pick(core)
        for t in range(1, narrows):
            total = total + to_core(pick(core ^ t), t)
        return total

    def sum_members(pick):
        total = pick(0)
        for s in range(1, group):
            total = total + to_member(pick(s), s)
        return total

    own = [block(out_weight, member ^ s, features, 1) for s in members]
    down_own = [block(side_down.T, member ^ s, features, 1) for s in members]
    stay_own = [block(residual, member ^ s, features, 1) for s in members]
    gain = block(ln_gain, member, features, 0)[None, :]
    columns = down_own[0].shape[0]
    side_rows = group * local

    def in_plane(downs):
        value = jnp.zeros((group * columns, features), BF16)
        for s in members:
            value = lax.dynamic_update_slice_in_dim(value, downs[s], (member ^ s) * columns, 0)
        return value

    if short:
        own = [jnp.concatenate(pair, axis=0) for pair in zip(own, down_own)]

        def line(value, pairs):
            pairs = [(i * group + m, j * group + m) for i, j in pairs for m in members]
            return lax.ppermute(value, "wide", pairs)

        outward, inward = [(1, 0), (2, 3)], [(1, 2), (2, 1)]

        def step_one(value):
            return line(value, outward + [(0, 1), (3, 2)]), line(value, inward)

        def step_two(first, second):
            return line(first, inward), line(second, outward)

        own_one = step_one(own[0])
        own_two = step_two(*own_one)
        rest = jnp.concatenate([to_member(own[s], s) for s in range(1, group)], axis=0)

        rest_one = step_one(rest)
        _, context, stay_own, own_two = lax.optimization_barrier((rest, context, stay_own, own_two))
        boxes = [jnp.concatenate([context, value], axis=1) for value in stay_own[1:]]
        own_last = line(own_two[0], outward)
        arrived = [to_member(boxes[0], 1), to_member(boxes[1], 2)]

        rest_two = step_two(*rest_one)
        arrived, boxes, _, own_last = lax.optimization_barrier((arrived, boxes, rest_one, own_last))
        arrived.append(to_member(boxes[2], 3))
        heads = context.shape[1]
        part = jnp.concatenate([context] + [v[:, :heads] for v in arrived[:2]] + [jnp.zeros_like(context)], axis=0)
        stay = stay_own[:1] + [v[:, heads:] for v in arrived[:2]]

        box, part, stay, rest_two = lax.optimization_barrier((arrived[2], part, stay, rest_two))
        rest_last = line(rest_two[0], outward)
        part = lax.dynamic_update_slice_in_dim(part, box[:, :heads], 3 * tokens, 0)
        stay.append(box[:, heads:])
        mine, other = [v.reshape(group, tokens, -1) for v in (part, to_core(part, 1))]
        flow = [own[0], rest]
        for pair in zip(own_one + own_two, rest_one + rest_two):
            flow += pair
        total, near_down = attend(rows, planes, mine, other, stay, flow)
        last = jnp.where(plane == 0, planes - 1, 0)
        width = group * rows
        last_part = jnp.where(last * width // heads == core, mine, other)
        last_part = lax.dynamic_slice_in_dim(last_part, last * width % heads, width, 2)
        last_part = last_part.reshape(group, narrows, local, width).swapaxes(0, 1).reshape(-1, width)
        flow = [own_last, rest_last]
        keep, send = finish(rows, planes, total, last_part, gain, near_down, flow)
        summed = keep + to_core(send, 1)
        span = local + 8
        pieces = [summed[:span]]
        pieces += [to_member(summed[s * span : (s + 1) * span], s) for s in range(1, group)]
        width = out_weight.shape[1] * narrows
        all_tokens = local * wides * narrows
        side_out, keep, send = side_block(width, all_tokens, pieces, f_weight, g_weight, targets)
        grads = keep + to_core(send, 1)
    else:
        pieces = [to_member(own[s], s) for s in members]
        down_plane = in_plane([to_member(down_own[s], s) for s in members])
        arrived = [to_member(context, s) for s in members]
        stay = [to_member(stay_own[s], s) for s in members]
        parts = [to_core(jnp.concatenate(arrived, axis=0), t) for t in cores]
        lines = [[p * group + m for p in range(planes)] for m in range(group)]
        chunk = jnp.zeros((group * rows, features), BF16)
        for s in members:
            chunk = lax.dynamic_update_slice_in_dim(chunk, pieces[s], (member ^ s) * rows, 0)
        weight = lax.all_gather(chunk, "wide", axis_index_groups=lines, tiled=True)
        all_down = lax.all_gather(down_plane, "wide", axis_index_groups=lines, tiled=True)

        def by_core(value):
            value = value.reshape(group, narrows, local, -1)
            return value.swapaxes(0, 1).reshape(group * tokens, -1)

        heads = context.shape[1]
        attn_sum = jnp.zeros((), F32)
        for t in cores:
            share = block(weight, core ^ t, heads, 0)
            attn_sum = attn_sum + jnp.dot(parts[t], share, preferred_element_type=F32)
        stream = (jnp.concatenate(stay, axis=0).astype(F32) + attn_sum).astype(BF16)
        stream = by_core(stream).astype(F32)
        scaled = (stream * gain.astype(F32)).astype(BF16).reshape(narrows, side_rows, features)
        gains = jnp.broadcast_to(gain[None], (narrows, 8, features))
        scaled = jnp.concatenate([scaled, gains], axis=1)
        stats = jnp.stack([jnp.sum(stream, axis=1), jnp.sum(stream * stream, axis=1)])
        stats_own = stats.reshape(2, narrows, group, local)

        def share_of_core(k):
            lhs = lax.dynamic_index_in_dim(scaled, k, 0, keepdims=False)
            return lax.dot_general(lhs, all_down, (((1,), (1,)), ((), ())), preferred_element_type=F32)

        summed = sum_cores(share_of_core)
        tail = summed[side_rows:]
        projected = sum_members(
            lambda s: jnp.concatenate([summed[s * local : (s + 1) * local], tail], axis=0)
        )
        summed_stats = sum_cores(lambda k: lax.dynamic_index_in_dim(stats_own, k, 1, keepdims=False))
        stats = sum_members(lambda s: summed_stats[:, s])
        projected, gain_map = projected[:local], projected[local]

        width = out_weight.shape[1] * narrows
        mean = stats[0] / width
        spread = stats[1] / width - mean * mean
        side_in = (projected - mean[:, None] * gain_map[None, :]) / jnp.sqrt(spread + 1e-06)[:, None]
        half = side_in.shape[1] // 2
        f_w, g_w = f_weight.astype(F32), g_weight.astype(F32)
        first, second = side_in[:, :half], side_in[:, half:]
        f_value, f_pull = jax.vjp(coupling, second, f_w)
        upper = first + f_value
        g_value, g_pull = jax.vjp(coupling, upper, g_w)
        lower = second + g_value
        side_out = jnp.concatenate([upper, lower], axis=1)
        misfit = (side_out - targets) / (local * wides * narrows)
        upper_back, g_local = g_pull(misfit[:, half:])
        f_local = f_pull(misfit[:, :half] + upper_back)[1]
        f_total, g_total = lax.psum((f_local, g_local), ("wide", "narrow"))
        return side_out, f_total, g_total

    half = grads.shape[1]
    share = grads.shape[0] // group
    part = grads
    grads = sum_members(lambda s: block(part, member ^ s, share, 0))
    share = share // planes

    def shift(value, k):
        return lax.ppermute(value, "wide", [(i, (i + k * group) % wides) for i in range(wides)])

    part = grads
    grads = block(part, plane, share, 0)
    for k in range(1, planes):
        grads = grads + shift(block(part, (plane + k) % planes, share, 0), k)
    whole = jnp.zeros((planes * share, half), F32)
    for k in range(planes):
        piece = shift(grads, k) if k else grads
        whole = lax.dynamic_update_slice_in_dim(whole, piece, (plane - k) % planes * share, 0)
    share = share * planes
    part, whole = whole, jnp.zeros((group * share, half), F32)
    for s in members:
        whole = lax.dynamic_update_slice_in_dim(whole, to_member(part, s), (member ^ s) * share, 0)
    other = to_core(whole, 1)
    return side_out, jnp.where(core == 0, whole, other), jnp.where(core == 0, other, whole)


def solution(mesh):
    wides, narrows = mesh.shape["wide"], mesh.shape["narrow"]
    group = GROUP if wides % GROUP == 0 else 1
    in_specs = (
        P("wide", "narrow"),
        P("wide", "narrow"),
        P("wide", "narrow"),
        P("narrow"),
        P("narrow", "wide"),
        P(),
        P(),
        P(("wide", "narrow"), None),
    )
    out_specs = (P(("wide", "narrow"), None), P(), P())
    return jax.shard_map(
        functools.partial(per_device, group, wides, narrows),
        mesh=mesh,
        in_specs=in_specs,
        out_specs=out_specs,
        check_vma=False,
    )
```

```python
import functools

import jax
import jax.numpy as jnp
from jax import lax
from jax.experimental import pallas as pl
from jax.experimental.pallas import tpu as pltpu
from jax.sharding import PartitionSpec as P

HIGH = lax.Precision.HIGH
F32 = jnp.float32
BF16 = jnp.bfloat16
GROUP = 4


def coupling(values, weight):
    return jax.nn.gelu(jnp.dot(values, weight, precision=HIGH))


def place():
    wide, core = lax.axis_index("wide"), lax.axis_index("narrow")
    return wide // GROUP, wide % GROUP, core


ROUTES = ((0, 1, 4, 5), (1, 0, 2, 3), (3, 2, 0, 1), (5, 4, 1, 0))
LAST = 5


def part_of(flow, at, p):
    return flow[2 * ROUTES[at][p] :][:2]


def share_of(pair, s, start, count, span):
    at = start + (s - 1) * span if s else start
    return pair[1 if s else 0].at[pl.ds(at, count)]


def attend_kernel(rows, planes, *refs):
    mine_ref, other_ref, *refs = refs
    stay_refs, (*flow, out_ref, down_ref, weight, sems, down_sems) = refs[:GROUP], refs[GROUP:]
    plane, member, core = place()
    span = flow[0].shape[0]
    columns = span - rows

    for at in range(planes):

        @pl.when((pl.program_id(0) == 0) & (plane == at))
        def _():
            copies = []
            for p in range(planes):
                if ROUTES[at][p] == LAST:
                    weight[p * GROUP * rows : (p + 1) * GROUP * rows] = jnp.zeros((GROUP * rows, weight.shape[1]), BF16)
                    ends = (p * GROUP * columns, (p + 1) * GROUP * columns)
                    down_ref[ends[0] : ends[1]] = jnp.zeros((GROUP * columns, weight.shape[1]), BF16)
                    continue
                for s in range(GROUP):
                    target = pl.multiple_of((p * GROUP + (member ^ s)) * rows, 64)
                    source = share_of(part_of(flow, at, p), s, 0, rows, span)
                    copies.append(pltpu.make_async_copy(source, weight.at[pl.ds(target, rows)], sems.at[p, s]))
                    target = pl.multiple_of((p * GROUP + (member ^ s)) * columns, 16)
                    source = share_of(part_of(flow, at, p), s, rows, columns, span)
                    target = down_ref.at[pl.ds(target, columns)]
                    copies.append(pltpu.make_async_copy(source, target, down_sems.at[p, s]))
            for copy in copies:
                copy.start()
            for copy in copies:
                copy.wait()

    group, local, heads = mine_ref.shape
    for h in range(0, group, 2):
        lhs = mine_ref[h : h + 2].reshape(2 * local, heads)
        rhs = other_ref[h : h + 2].reshape(2 * local, heads)
        at = pl.multiple_of(core * heads, 128)
        total = jnp.dot(lhs, weight[pl.ds(at, heads)], preferred_element_type=F32)
        at = pl.multiple_of((1 - core) * heads, 128)
        total += jnp.dot(rhs, weight[pl.ds(at, heads)], preferred_element_type=F32)
        for g in range(2):
            stay = stay_refs[h + g][...].astype(F32)
            out_ref[(h + g) * local : (h + g + 1) * local] = stay + total[g * local : (g + 1) * local]


def attend(rows, planes, mine, other, stay, flow):
    group, tokens, heads = mine.shape
    count = flow[0].shape[1]
    part = pl.BlockSpec((group, tokens // 2, heads), lambda i: (0, i, 0))
    out = (flow[0].shape[0] - rows) * group * planes
    return pl.pallas_call(
        functools.partial(attend_kernel, rows, planes),
        grid=(2,),
        in_specs=[part, part]
        + [pl.BlockSpec((tokens // 2, count), lambda i: (i, 0))] * group
        + [pl.BlockSpec(memory_space=pl.ANY)] * len(flow),
        out_specs=[
            pl.BlockSpec((group * tokens // 2, count), lambda i: (i, 0)),
            pl.BlockSpec((out, count), lambda i: (0, 0)),
        ],
        out_shape=[
            jax.ShapeDtypeStruct((group * tokens, count), F32),
            jax.ShapeDtypeStruct((out, count), BF16),
        ],
        scratch_shapes=[
            pltpu.VMEM((2 * heads, count), BF16),
            pltpu.SemaphoreType.DMA((planes, group)),
            pltpu.SemaphoreType.DMA((planes, group)),
        ],
        compiler_params=pltpu.CompilerParams(vmem_limit_bytes=26 << 20),
        cost_estimate=pl.CostEstimate(
            flops=4 * group * tokens * heads * count, bytes_accessed=16 << 20, transcendentals=0
        ),
    )(mine, other, *stay, *flow)


def finish_kernel(rows, planes, *refs):
    total_ref, far_ref, gain_ref, near_ref, *flow, keep_ref, send_ref, weight, down, sems, down_sems, near_sem = refs
    plane, member, core = place()
    span = flow[0].shape[0]
    columns = span - rows

    def far_copies():
        out = []
        for s in range(GROUP):
            target = pl.multiple_of((member ^ s) * rows, 64)
            source = share_of(flow, s, 0, rows, span)
            out.append(pltpu.make_async_copy(source, weight.at[pl.ds(target, rows)], sems.at[s]))
        return out

    def down_copies(p):
        out = []
        for s in range(GROUP):
            target = pl.multiple_of((p * GROUP + (member ^ s)) * columns, 16)
            source = share_of(flow, s, rows, columns, span)
            out.append(pltpu.make_async_copy(source, down.at[pl.ds(target, columns)], down_sems.at[s]))
        return out

    near = pltpu.make_async_copy(near_ref, down, near_sem)
    near.start()
    far = far_copies()
    for copy in far:
        copy.start()
    near.wait()
    ends = [(at, ROUTES[at].index(LAST)) for at in range(planes) if LAST in ROUTES[at]]
    for at, p in ends:

        @pl.when(plane == at)
        def _():
            for copy in down_copies(p):
                copy.start()

    for copy in far:
        copy.wait()
    gain = gain_ref[...].astype(F32)
    half = total_ref.shape[0] // 2
    local = half // GROUP
    line = local + 8
    dims = (((1,), (1,)), ((), ()))
    gains = None
    for out_ref, k in ((send_ref, 1 - core), (keep_ref, core)):
        for h in range(0, GROUP, 2):
            own_rows = pl.ds(pl.multiple_of(k * half + h * local, 128), 2 * local)
            total = total_ref[own_rows] + jnp.dot(far_ref[own_rows], weight[...], preferred_element_type=F32)
            stream = total.astype(BF16).astype(F32)
            row_sum = jnp.sum(stream, axis=1, keepdims=True)
            squares = jnp.sum(stream * stream, axis=1, keepdims=True)
            lane = lax.broadcasted_iota(jnp.int32, (2 * local, 128), 1)
            both = jnp.where(lane == 0, row_sum, jnp.where(lane == 1, squares, 0.0)).T
            if gains is None:
                for at, p in ends:

                    @pl.when(plane == at)
                    def _():
                        for copy in down_copies(p):
                            copy.wait()

                gains = jnp.broadcast_to(gain_ref[...], (16, gain_ref.shape[1]))
                gains = lax.dot_general(gains, down[...], dims, preferred_element_type=F32)[:8]
            scaled = (stream * gain).astype(BF16)
            value = lax.dot_general(scaled, down[...], dims, preferred_element_type=F32)
            for g in range(2):
                at = (h + g) * line
                out_ref[at : at + local] = value[g * local : (g + 1) * local]
                out_ref[at + local : at + line] = gains
                out_ref[at + local + 1 : at + local + 3, :local] = both[:2, g * local : (g + 1) * local]


def finish(rows, planes, total, far, gain, near, flow):
    count = total.shape[1]
    tokens = total.shape[0]
    span = flow[0].shape[0]
    out = (span - rows) * GROUP * planes
    inside = pl.BlockSpec(memory_space=pltpu.VMEM)
    return pl.pallas_call(
        functools.partial(finish_kernel, rows, planes),
        in_specs=[inside] * 4 + [pl.BlockSpec(memory_space=pl.ANY)] * len(flow),
        out_specs=[inside, inside],
        out_shape=[jax.ShapeDtypeStruct((tokens // 2 + 8 * GROUP, out), F32)] * 2,
        scratch_shapes=[
            pltpu.VMEM((GROUP * rows, count), BF16),
            pltpu.VMEM((out, count), BF16),
            pltpu.SemaphoreType.DMA((GROUP,)),
            pltpu.SemaphoreType.DMA((GROUP,)),
            pltpu.SemaphoreType.DMA,
        ],
        compiler_params=pltpu.CompilerParams(vmem_limit_bytes=20 << 20),
        cost_estimate=pl.CostEstimate(
            flops=2 * tokens * count * (GROUP * rows + out), bytes_accessed=16 << 20, transcendentals=0
        ),
    )(total, far, gain, near, *flow)


def split(value):
    high = value.astype(BF16)
    return high, (value - high.astype(F32)).astype(BF16)


def times(value, weight, turned=False):
    count = value.shape[0]
    dims = (((1,), (1 if turned else 0,)), ((), ()))
    both = lax.dot_general(jnp.concatenate(split(value), axis=0), weight, dims, preferred_element_type=F32)
    return both[:count] + both[count:]


def outer(left, right):
    (left, left_low), (right, right_low) = split(left), split(right)
    left = jnp.concatenate([left, left, left_low], axis=0)
    right = jnp.concatenate([right, right_low, right], axis=0)
    return lax.dot_general(left, right, (((0,), (0,)), ((), ())), preferred_element_type=F32)


def gelu_and_slope(v):
    scale = 0.7978845608028654
    t = jnp.tanh(scale * (v + 0.044715 * (v * v * v)))
    slope = 0.5 * (1.0 + t) + 0.5 * v * (1.0 - t * t) * (scale * (1.0 + 3.0 * 0.044715 * (v * v)))
    return 0.5 * v * (1.0 + t), slope


def side_kernel(width, all_tokens, *refs):
    *part_refs, f_ref, g_ref, target_ref, out_ref, keep_ref, send_ref = refs
    local, features = out_ref.shape
    half = features // 2
    total = part_refs[0][...]
    for ref in part_refs[1:]:
        total = total + ref[...]
    tail = total[local:]
    stats = jnp.concatenate([tail[:, :local]] * (local // 8), axis=0).T
    mean = stats[:, 1:2] / width
    spread = stats[:, 2:3] / width - mean * mean
    side_in = (total[:local] - mean * tail[:1]) / jnp.sqrt(spread + 1e-06)
    first, second = side_in[:, :half], side_in[:, half:]
    f_w, g_w = f_ref[...], g_ref[...]
    f_value, f_slope = gelu_and_slope(times(second, f_w))
    upper = first + f_value
    g_value, g_slope = gelu_and_slope(times(upper, g_w))
    lower = second + g_value
    out_ref[:, :half] = upper
    out_ref[:, half:] = lower
    g_back = (lower - target_ref[:, half:]) / all_tokens * g_slope
    upper_back = (upper - target_ref[:, :half]) / all_tokens + times(g_back, g_w, turned=True)
    g_grad = outer(upper, g_back)
    f_grad = outer(second, upper_back * f_slope)
    core = lax.axis_index("narrow")

    @pl.when(core == 0)
    def _():
        keep_ref[...] = f_grad
        send_ref[...] = g_grad

    @pl.when(core != 0)
    def _():
        keep_ref[...] = g_grad
        send_ref[...] = f_grad


def side_block(width, all_tokens, parts, f_weight, g_weight, targets):
    inside = pl.BlockSpec(memory_space=pltpu.VMEM)
    grad = jax.ShapeDtypeStruct(f_weight.shape, F32)
    work = targets.shape[0] * f_weight.size
    return pl.pallas_call(
        functools.partial(side_kernel, width, all_tokens),
        in_specs=[inside] * (len(parts) + 3),
        out_specs=[inside] * 3,
        out_shape=[jax.ShapeDtypeStruct(targets.shape, F32), grad, grad],
        compiler_params=pltpu.CompilerParams(vmem_limit_bytes=24 << 20),
        cost_estimate=pl.CostEstimate(flops=24 * work, bytes_accessed=5 << 20, transcendentals=2 * targets.size),
    )(*parts, f_weight, g_weight, targets)


def per_device(group, wides, narrows, context, out_weight, residual, ln_gain, side_down, f_weight, g_weight, targets):
    planes = wides // group
    wide, core = lax.axis_index("wide"), lax.axis_index("narrow")
    plane, member = wide // group, wide % group
    short = group == GROUP and planes == 4 and narrows == 2
    features = out_weight.shape[1] // group
    rows = out_weight.shape[0]
    tokens = context.shape[0]
    local = tokens // narrows
    members = range(group)
    cores = range(narrows)

    def to_member(value, s):
        pairs = [(i, i - i % group + (i % group ^ s)) for i in range(wides)]
        return lax.ppermute(value, "wide", pairs) if s else value

    def to_core(value, t):
        return lax.ppermute(value, "narrow", [(i, i ^ t) for i in range(narrows)]) if t else value

    def block(value, index, size, axis):
        return lax.dynamic_slice_in_dim(value, index * size, size, axis)

    def sum_cores(pick):
        total = pick(core)
        for t in range(1, narrows):
            total = total + to_core(pick(core ^ t), t)
        return total

    def sum_members(pick):
        total = pick(0)
        for s in range(1, group):
            total = total + to_member(pick(s), s)
        return total

    own = [block(out_weight, member ^ s, features, 1) for s in members]
    down_own = [block(side_down, member ^ s, features, 0).T for s in members]
    stay_own = [block(residual, member ^ s, features, 1) for s in members]
    gain = block(ln_gain, member, features, 0)[None, :]
    columns = down_own[0].shape[0]
    side_rows = group * local

    def in_plane(downs):
        value = jnp.zeros((group * columns, features), BF16)
        for s in members:
            value = lax.dynamic_update_slice_in_dim(value, downs[s], (member ^ s) * columns, 0)
        return value

    if short:
        own = [jnp.concatenate(pair, axis=0) for pair in zip(own, down_own)]

        def line(value, pairs):
            pairs = [(i * group + m, j * group + m) for i, j in pairs for m in members]
            return lax.ppermute(value, "wide", pairs)

        outward, inward = [(1, 0), (2, 3)], [(1, 2), (2, 1)]

        def step_one(value):
            return line(value, outward + [(0, 1), (3, 2)]), line(value, inward)

        def step_two(first, second):
            return line(first, inward), line(second, outward)

        own_one = step_one(own[0])
        own_two = step_two(*own_one)
        rest = jnp.concatenate([to_member(own[s], s) for s in range(1, group)], axis=0)

        rest_one = step_one(rest)
        _, context, stay_own, own_two = lax.optimization_barrier((rest, context, stay_own, own_two))
        boxes = [jnp.concatenate([context, value], axis=1) for value in stay_own[1:]]
        own_last = line(own_two[0], outward)
        arrived = [to_member(boxes[0], 1), to_member(boxes[1], 2)]

        rest_two = step_two(*rest_one)
        arrived, boxes, _, own_last = lax.optimization_barrier((arrived, boxes, rest_one, own_last))
        arrived.append(to_member(boxes[2], 3))
        heads = context.shape[1]
        part = jnp.concatenate([context] + [v[:, :heads] for v in arrived[:2]] + [jnp.zeros_like(context)], axis=0)
        stay = stay_own[:1] + [v[:, heads:] for v in arrived[:2]]

        box, part, stay, rest_two = lax.optimization_barrier((arrived[2], part, stay, rest_two))
        rest_last = line(rest_two[0], outward)
        part = lax.dynamic_update_slice_in_dim(part, box[:, :heads], 3 * tokens, 0)
        stay.append(box[:, heads:])
        mine, other = [v.reshape(group, tokens, -1) for v in (part, to_core(part, 1))]
        flow = [own[0], rest]
        for pair in zip(own_one + own_two, rest_one + rest_two):
            flow += pair
        total, near_down = attend(rows, planes, mine, other, stay, flow)
        last = jnp.where(plane == 0, planes - 1, 0)
        width = group * rows
        last_part = jnp.where(last * width // heads == core, mine, other)
        last_part = lax.dynamic_slice_in_dim(last_part, last * width % heads, width, 2)
        last_part = last_part.reshape(group, narrows, local, width).swapaxes(0, 1).reshape(-1, width)
        flow = [own_last, rest_last]
        keep, send = finish(rows, planes, total, last_part, gain, near_down, flow)
        summed = keep + to_core(send, 1)
        span = local + 8
        pieces = [summed[:span]]
        pieces += [to_member(summed[s * span : (s + 1) * span], s) for s in range(1, group)]
        width = out_weight.shape[1] * narrows
        all_tokens = local * wides * narrows
        side_out, keep, send = side_block(width, all_tokens, pieces, f_weight, g_weight, targets)
        grads = keep + to_core(send, 1)
    else:
        pieces = [to_member(own[s], s) for s in members]
        down_plane = in_plane([to_member(down_own[s], s) for s in members])
        arrived = [to_member(context, s) for s in members]
        stay = [to_member(stay_own[s], s) for s in members]
        parts = [to_core(jnp.concatenate(arrived, axis=0), t) for t in cores]
        lines = [[p * group + m for p in range(planes)] for m in range(group)]
        chunk = jnp.zeros((group * rows, features), BF16)
        for s in members:
            chunk = lax.dynamic_update_slice_in_dim(chunk, pieces[s], (member ^ s) * rows, 0)
        weight = lax.all_gather(chunk, "wide", axis_index_groups=lines, tiled=True)
        all_down = lax.all_gather(down_plane, "wide", axis_index_groups=lines, tiled=True)

        def by_core(value):
            value = value.reshape(group, narrows, local, -1)
            return value.swapaxes(0, 1).reshape(group * tokens, -1)

        heads = context.shape[1]
        attn_sum = jnp.zeros((), F32)
        for t in cores:
            share = block(weight, core ^ t, heads, 0)
            attn_sum = attn_sum + jnp.dot(parts[t], share, preferred_element_type=F32)
        stream = (jnp.concatenate(stay, axis=0).astype(F32) + attn_sum).astype(BF16)
        stream = by_core(stream).astype(F32)
        scaled = (stream * gain.astype(F32)).astype(BF16).reshape(narrows, side_rows, features)
        gains = jnp.broadcast_to(gain[None], (narrows, 8, features))
        scaled = jnp.concatenate([scaled, gains], axis=1)
        stats = jnp.stack([jnp.sum(stream, axis=1), jnp.sum(stream * stream, axis=1)])
        stats_own = stats.reshape(2, narrows, group, local)

        def share_of_core(k):
            lhs = lax.dynamic_index_in_dim(scaled, k, 0, keepdims=False)
            return lax.dot_general(lhs, all_down, (((1,), (1,)), ((), ())), preferred_element_type=F32)

        summed = sum_cores(share_of_core)
        tail = summed[side_rows:]
        projected = sum_members(
            lambda s: jnp.concatenate([summed[s * local : (s + 1) * local], tail], axis=0)
        )
        summed_stats = sum_cores(lambda k: lax.dynamic_index_in_dim(stats_own, k, 1, keepdims=False))
        stats = sum_members(lambda s: summed_stats[:, s])
        projected, gain_map = projected[:local], projected[local]

        width = out_weight.shape[1] * narrows
        mean = stats[0] / width
        spread = stats[1] / width - mean * mean
        side_in = (projected - mean[:, None] * gain_map[None, :]) / jnp.sqrt(spread + 1e-06)[:, None]
        half = side_in.shape[1] // 2
        f_w, g_w = f_weight.astype(F32), g_weight.astype(F32)
        first, second = side_in[:, :half], side_in[:, half:]
        f_value, f_pull = jax.vjp(coupling, second, f_w)
        upper = first + f_value
        g_value, g_pull = jax.vjp(coupling, upper, g_w)
        lower = second + g_value
        side_out = jnp.concatenate([upper, lower], axis=1)
        misfit = (side_out - targets) / (local * wides * narrows)
        upper_back, g_local = g_pull(misfit[:, half:])
        f_local = f_pull(misfit[:, :half] + upper_back)[1]
        f_total, g_total = lax.psum((f_local, g_local), ("wide", "narrow"))
        return side_out, f_total, g_total

    half = grads.shape[1]
    share = grads.shape[0] // group
    part = grads
    grads = sum_members(lambda s: block(part, member ^ s, share, 0))
    share = share // planes

    def shift(value, k):
        return lax.ppermute(value, "wide", [(i, (i + k * group) % wides) for i in range(wides)])

    part = grads
    grads = block(part, plane, share, 0)
    for k in range(1, planes):
        grads = grads + shift(block(part, (plane + k) % planes, share, 0), k)
    whole = jnp.zeros((planes * share, half), F32)
    for k in range(planes):
        piece = shift(grads, k) if k else grads
        whole = lax.dynamic_update_slice_in_dim(whole, piece, (plane - k) % planes * share, 0)
    share = share * planes
    part, whole = whole, jnp.zeros((group * share, half), F32)
    for s in members:
        whole = lax.dynamic_update_slice_in_dim(whole, to_member(part, s), (member ^ s) * share, 0)
    other = to_core(whole, 1)
    return side_out, jnp.where(core == 0, whole, other), jnp.where(core == 0, other, whole)


def solution(mesh):
    wides, narrows = mesh.shape["wide"], mesh.shape["narrow"]
    group = GROUP if wides % GROUP == 0 else 1
    in_specs = (
        P("wide", "narrow"),
        P("wide", "narrow"),
        P("wide", "narrow"),
        P("narrow"),
        P("narrow", "wide"),
        P(),
        P(),
        P(("wide", "narrow"), None),
    )
    out_specs = (P(("wide", "narrow"), None), P(), P())
    return jax.shard_map(
        functools.partial(per_device, group, wides, narrows),
        mesh=mesh,
        in_specs=in_specs,
        out_specs=out_specs,
        check_vma=False,
    )
```
